128 devices in a mesh: gx: 16 (over z, y), gy: 8 (over x, core).
Axes of the slice: x: 4, y: 4, z: 4, core: 2. Of those that a mesh axis runs over, the one named last changes fastest.
Arguments:
- adjoint_in: float32 [4, 48, 128, 1024], P(None, None, 'gx', 'gy'), may hold values from -6 to 6
- conc: float32 [4, 48, 128, 1024], P(None, None, 'gx', 'gy'), may hold values from 0 to 1
- pressure: float32 [48, 128, 1024], P(None, 'gx', 'gy'), may hold values from -3 to 3
- perm: float32 [48, 128, 1024], P(None, 'gx', 'gy'), may hold values from 0.3 to 3
- porosity: float32 [48, 128, 1024], P(None, 'gx', 'gy'), may hold values from 0.2 to 0.4
- storage: float32 [48, 128, 1024], P(None, 'gx', 'gy'), may hold values from 0.5 to 2
- rock: int32 [48, 128, 1024], P(None, 'gx', 'gy'), may hold values from 0 to 7
- upwind: int32 [4, 48, 128, 1024], P(None, None, 'gx', 'gy'), may hold values from 0 to 1, as said below
- sorption: float32 [2, 8, 4], replicated, may hold values from 0.3 to 3
Outputs:
- adjoint_out: float32 [4, 48, 128, 1024], P(None, None, 'gx', 'gy')
- grad: float32 [48, 128, 1024], P(None, 'gx', 'gy')
The draws below stay inside these ranges and needn't reach their ends.
Inputs may be any that keep to these rules, and one draw needn't show every extreme that they name: upwind[0] and upwind[1] flag a cell's faces toward lower and higher first horizontal index, upwind[2] and upwind[3] toward lower and higher second index; a flag of 1 means the cell of lower index on that face is upwind. upwind[1] of a cell equals upwind[0] of the next cell along the first dimension, and upwind[3] equals upwind[2] of the next cell along the second. Flags on the outer boundary of the grid are arbitrary.
All inputs are finite; a program needn't handle non-finite values.
Results may differ from the reference program's by a relative error of at most 0.0003.
Values sent between devices are 32-bit elements; how exact they have to be, the bound alone decides.
A program may use at most 256 MiB of HBM per device.

```python
import math
import jax
import jax.numpy as jnp

SPEC = 4
ROCKS = 8
NZ = 48
SUB = 8
CHEB = 4
NX = 128
NY = 1024


def draw_upwind(key, part):
    faces_east = jax.random.randint(jax.random.fold_in(key, 11), (NZ, NX + 1, NY), 0, 2, dtype=jnp.int32)
    faces_north = jax.random.randint(jax.random.fold_in(key, 23), (NZ, NX, NY + 1), 0, 2, dtype=jnp.int32)
    stacked = jnp.stack([faces_east[:, :-1, :], faces_east[:, 1:, :], faces_north[:, :, :-1], faces_north[:, :, 1:]])
    return stacked.astype(jnp.int32)


def touch_ends(values, key, smallest, top_value):
    spot = [jax.random.randint(jax.random.fold_in(key, axis), (), 0, length) for axis, length in enumerate(values.shape)]
    main_axis = values.shape.index(max(values.shape))
    next_to = spot[:main_axis] + [(spot[main_axis] + 1) % values.shape[main_axis]] + spot[main_axis + 1:]
    return values.at[tuple(spot)].set(smallest).at[tuple(next_to)].set(top_value)


def block_scale(own_key, dims, split, least, high):
    def one(axis_at, shards_of):
        draws = jax.random.uniform(jax.random.fold_in(jax.random.fold_in(own_key, 6), axis_at), (shards_of,), jnp.float32, least / len(split), high / len(split))
        return jnp.repeat(jnp.exp(draws), dims[axis_at] // shards_of).reshape((-1,) + (1,) * (len(dims) - axis_at - 1))

    level = one(*split[0])
    for cut in split[1:]:
        level = level * one(*cut)
    return level


def centred(own_key, dims, spread, bound, shards=(), held_as=jnp.bfloat16):
    factor_of = block_scale(own_key, dims, shards, -0.22, 0.18) if shards else 1.0
    drawn = jax.random.normal(own_key, dims, jnp.float32) * spread * factor_of
    return jnp.minimum(jnp.maximum(drawn, -bound), bound).astype(held_as)


def setup_inputs(seed: int = 0) -> dict:
    keys = jax.random.split(jax.random.key(seed), 10)
    return {
        "adjoint_in": centred(keys[0], (SPEC, NZ, NX, NY), 1.0, 6.0, ((2, 16), (3, 8)), jnp.float32),
        "conc": jnp.clip(1.0 * jax.random.uniform(keys[1], (SPEC, NZ, NX, NY), jnp.float32) ** block_scale(keys[1], (SPEC, NZ, NX, NY), ((2, 16), (3, 8)), -0.2, 0.2), 0.0, 1.0),
        "pressure": centred(keys[2], (NZ, NX, NY), 0.5, 3.0, ((1, 16), (2, 8)), jnp.float32),
        "perm": jnp.clip(jnp.exp(math.log(3.0) - 2.3025851 * jax.random.uniform(keys[3], (NZ, NX, NY), jnp.float32) ** block_scale(keys[3], (NZ, NX, NY), ((1, 16), (2, 8)), -0.2, 0.2)), 0.3, 3.0),
        "porosity": jnp.clip(0.2 + 0.2 * jax.random.uniform(keys[4], (NZ, NX, NY), jnp.float32) ** block_scale(keys[4], (NZ, NX, NY), ((1, 16), (2, 8)), -0.2, 0.2), 0.2, 0.4),
        "storage": jnp.clip(jnp.exp(math.log(2.0) - 1.3862944 * jax.random.uniform(keys[5], (NZ, NX, NY), jnp.float32) ** block_scale(keys[5], (NZ, NX, NY), ((1, 16), (2, 8)), -0.2, 0.2)), 0.5, 2.0),
        "rock": touch_ends(jax.random.randint(keys[6], (NZ, NX, NY), 0, ROCKS), jax.random.fold_in(keys[6], 1), 0, ROCKS - 1).astype(jnp.int32),
        "upwind": draw_upwind(jax.random.fold_in(keys[9], 71), 0),
        "sorption": jnp.clip(jnp.exp(jax.random.uniform(keys[8], (2, ROCKS, SPEC), jnp.float32, math.log(0.3), math.log(3.0))), 0.3, 3.0),
    }


step_size = 0.02
contract = 0.9


def harmonic(left, right):
    total = left + right
    return 2.0 * left * right / jnp.where(total > 0, total, 1.0)


def harm_slope(left, right):
    total = left + right
    safe = jnp.where(total > 0, total, 1.0)
    return 2.0 * right * right / (safe * safe)


def east_pairs(field):
    return field[..., :-1, 1:-1], field[..., 1:, 1:-1]


def north_pairs(field):
    return field[..., 1:-1, :-1], field[..., 1:-1, 1:]


def vertical_pairs(field):
    padded = jnp.pad(field, ((1, 1), (0, 0), (0, 0)))
    return padded[:-1], padded[1:]


def pad_plane(field):
    widths = [(0, 0)] * (field.ndim - 2) + [(1, 1), (1, 1)]
    return jnp.pad(field, widths)


def operate(field_pad, perm_pad, store):
    inner = field_pad[..., 1:-1, 1:-1]
    perm_in = perm_pad[..., 1:-1, 1:-1]
    perm_left, perm_right = east_pairs(perm_pad)
    val_left, val_right = east_pairs(field_pad)
    flow_east = harmonic(perm_left, perm_right) * (val_left - val_right)
    perm_left, perm_right = north_pairs(perm_pad)
    val_left, val_right = north_pairs(field_pad)
    flow_north = harmonic(perm_left, perm_right) * (val_left - val_right)
    perm_low, perm_high = vertical_pairs(perm_in)
    val_low, val_high = vertical_pairs(inner)
    flow_up = harmonic(perm_low, perm_high) * (val_low - val_high)
    return (store * inner + flow_east[:, 1:, :] - flow_east[:, :-1, :]
            + flow_north[:, :, 1:] - flow_north[:, :, :-1] + flow_up[1:] - flow_up[:-1])


def diagonal(perm_pad, store):
    perm_in = perm_pad[..., 1:-1, 1:-1]
    trans_east = harmonic(*east_pairs(perm_pad))
    trans_north = harmonic(*north_pairs(perm_pad))
    trans_up = harmonic(*vertical_pairs(perm_in))
    return (store + trans_east[:, 1:, :] + trans_east[:, :-1, :]
            + trans_north[:, :, 1:] + trans_north[:, :, :-1] + trans_up[1:] + trans_up[:-1])


def reference(adjoint_in, conc, pressure, perm, porosity, storage, rock, upwind, sorption):
    langmuir = jnp.zeros_like(conc)
    capacity = jnp.zeros_like(conc)
    for index in range(ROCKS):
        chosen = (rock == index)[None]
        langmuir = jnp.where(chosen, sorption[0, index][:, None, None, None], langmuir)
        capacity = jnp.where(chosen, sorption[1, index][:, None, None, None], capacity)
    area = porosity[None] * (1.0 + capacity * langmuir / jnp.square(1.0 + langmuir * conc))
    press_near = pad_plane(pressure)
    perm_near = pad_plane(perm)
    conc_near = pad_plane(conc)
    trans_east = harmonic(*east_pairs(perm_near))
    trans_north = harmonic(*north_pairs(perm_near))
    press_left, press_right = east_pairs(press_near)
    drop_east = press_left - press_right
    press_left, press_right = north_pairs(press_near)
    drop_north = press_left - press_right
    flux_east = trans_east * jnp.abs(drop_east)
    flux_north = trans_north * jnp.abs(drop_north)
    flag_east = jnp.concatenate([upwind[0], upwind[1][:, -1:, :]], axis=1).astype(jnp.float32)
    flag_north = jnp.concatenate([upwind[2], upwind[3][:, :, -1:]], axis=2).astype(jnp.float32)
    conc_left, conc_right = east_pairs(conc_near)
    upstream_east = flag_east * conc_left + (1.0 - flag_east) * conc_right
    conc_left, conc_right = north_pairs(conc_near)
    upstream_north = flag_north * conc_left + (1.0 - flag_north) * conc_right
    adjoint = adjoint_in
    grad_east = jnp.zeros_like(trans_east)
    grad_north = jnp.zeros_like(trans_north)
    for step in range(SUB):
        weighted_pad = pad_plane(adjoint / area)
        weight_left, weight_right = east_pairs(weighted_pad)
        diff_east = step_size * (weight_right - weight_left)
        weight_left, weight_right = north_pairs(weighted_pad)
        diff_north = step_size * (weight_right - weight_left)
        grad_east = grad_east + jnp.sum(upstream_east * diff_east, axis=0)
        grad_north = grad_north + jnp.sum(upstream_north * diff_north, axis=0)
        push_east = flux_east * diff_east
        push_north = flux_north * diff_north
        adjoint = (adjoint + (flag_east * push_east)[..., 1:, :] - ((1.0 - flag_east) * push_east)[..., :-1, :]
                   + (flag_north * push_north)[..., 1:] - ((1.0 - flag_north) * push_north)[..., :-1])
    source_east = trans_east * jnp.sign(drop_east) * grad_east
    source_north = trans_north * jnp.sign(drop_north) * grad_north
    source = (source_east[:, 1:, :] - source_east[:, :-1, :]
              + source_north[:, :, 1:] - source_north[:, :, :-1])
    diag_local = diagonal(perm_near, storage)
    residue = source / diag_local
    direction = residue
    multiplier = direction
    ratio_now = contract
    for step in range(CHEB - 1):
        image = operate(pad_plane(direction), perm_near, storage)
        residue = residue - image / diag_local
        ratio_next = 1.0 / (2.0 / contract - ratio_now)
        direction = ratio_next * ratio_now * direction + (2.0 * ratio_next / contract) * residue
        multiplier = multiplier + direction
        ratio_now = ratio_next
    mult_pad = pad_plane(multiplier)
    mult_left, mult_right = east_pairs(mult_pad)
    excess_east = jnp.abs(drop_east) * grad_east - (mult_left - mult_right) * drop_east
    mult_left, mult_right = north_pairs(mult_pad)
    excess_north = jnp.abs(drop_north) * grad_north - (mult_left - mult_right) * drop_north
    perm_left, perm_right = east_pairs(perm_near)
    grad = (harm_slope(perm_left, perm_right) * excess_east)[:, 1:, :] + (harm_slope(perm_right, perm_left) * excess_east)[:, :-1, :]
    perm_left, perm_right = north_pairs(perm_near)
    grad = grad + (harm_slope(perm_left, perm_right) * excess_north)[:, :, 1:] + (harm_slope(perm_right, perm_left) * excess_north)[:, :, :-1]
    perm_low, perm_high = vertical_pairs(perm)
    mult_low, mult_high = vertical_pairs(multiplier)
    press_low, press_high = vertical_pairs(pressure)
    excess_up = -(mult_low - mult_high) * (press_low - press_high)
    grad = grad + (harm_slope(perm_low, perm_high) * excess_up)[1:] + (harm_slope(perm_high, perm_low) * excess_up)[:-1]
    return adjoint, grad
```

```python
import jax
import jax.numpy as jnp
from jax import lax
from jax.experimental import pallas as pl
from jax.experimental.pallas import tpu as pltpu
from jax.sharding import PartitionSpec as P

ROCKS = 8
SUB = 8
CHEB = 4
SPEC = 4
NZ = 48
BX = 8
LANES = 128
ZT = NZ // 8
STEP = 0.02
CONTRACT = 0.9
F32 = jnp.float32
MESH = pl.DeviceIdType.MESH

CHEB_SLOT = SUB * SPEC
PERM_SLOT = CHEB_SLOT + CHEB
PRESS_SLOT = PERM_SLOT + 1
CONC_SLOT = PERM_SLOT + 2
SLOTS = PERM_SLOT + 3


def iota(shape, dim):
    return lax.broadcasted_iota(jnp.int32, shape, dim)


def pack_row(values, x, packed):
    pair = iota((8, LANES), 1) // 2
    for zt in range(ZT):
        t = x * ZT + zt
        turned = pltpu.roll(values[8 * zt:8 * zt + 8], 2 * t + 1, 1)
        packed = jnp.where(pair == t, turned, packed)
    return packed


def unpack_row(packed, x):
    tiles = []
    for zt in range(ZT):
        t = x * ZT + zt
        tiles.append(pltpu.roll(packed, LANES - 2 * t, 1) if t else packed)
    return jnp.concatenate(tiles, axis=0)


def align(left, right):
    even = iota((8, LANES), 1) % 2 == 0
    return jnp.where(even, left, pltpu.roll(right, LANES - 2, 1))


def kernel(adj_h, conc_h, press_h, perm_h, por_h, sto_h, rock_h, up_h, sorp, out_h, grad_h,
           adj, conc, press, perm, por, sto, rock, up, ia, w, wacc, py, hyl, hyr, hyw, pw,
           ps, psl, psr, coef, tau, st, kk, d, dpy, dhl, dhr, m, r, grad, in_sems, send, recv):
    gx = lax.axis_index("gx")
    gy = lax.axis_index("gy")
    nx = lax.axis_size("gx")
    ny = lax.axis_size("gy")
    to = [
        {"gx": lax.rem(gx + nx - 1, nx), "gy": gy},
        {"gx": lax.rem(gx + 1, nx), "gy": gy},
        {"gx": gx, "gy": lax.rem(gy + ny - 1, ny)},
        {"gx": gx, "gy": lax.rem(gy + 1, ny)},
    ]

    loads = {}

    def load(i, name, src, dst):
        loads[name] = []
        for x in range(BX):
            copy = pltpu.make_async_copy(src(x), dst(x), in_sems.at[i, x])
            copy.start()
            loads[name].append(copy)

    def arrived(*names):
        for name in names:
            for copy in loads[name]:
                copy.wait()

    barrier = pltpu.get_barrier_semaphore()
    for target in to:
        pl.semaphore_signal(barrier, inc=1, device_id=target, device_id_type=MESH)
    load(0, "conc", lambda x: conc_h.at[:, :, x, :], lambda x: conc.at[x + 1])
    load(1, "rock", lambda x: rock_h.at[:, x, :], lambda x: rock.at[x])
    load(2, "por", lambda x: por_h.at[:, x, :], lambda x: por.at[x])
    load(3, "adj", lambda x: adj_h.at[:, :, x, :], lambda x: adj.at[x])
    load(4, "perm", lambda x: perm_h.at[:, x, :], lambda x: perm.at[x + 1])
    load(5, "press", lambda x: press_h.at[:, x, :], lambda x: press.at[x + 1])
    load(6, "up", lambda x: up_h.at[:, :, x, :], lambda x: up.at[x])
    load(7, "sto", lambda x: sto_h.at[:, x, :], lambda x: sto.at[x])

    def message(slot, way, src, dst):
        return pltpu.make_async_remote_copy(
            src_ref=src, dst_ref=dst, send_sem=send.at[slot, way], recv_sem=recv.at[slot, way],
            device_id=to[way], device_id_type=MESH)

    def transport_messages(t, s):
        slot = t * SPEC + s
        return [
            message(slot, 0, w.at[t, 1, s], w.at[t, BX + 1, s]),
            message(slot, 1, w.at[t, BX, s], w.at[t, 0, s]),
            message(slot, 2, py.at[t, s], hyr.at[t, s]),
            message(slot, 3, py.at[t, s], hyl.at[t, s]),
        ]

    def cheb_messages(j):
        slot = CHEB_SLOT + j
        return [
            message(slot, 0, d.at[j, 1], d.at[j, BX + 1]),
            message(slot, 1, d.at[j, BX], d.at[j, 0]),
            message(slot, 2, dpy.at[j], dhr.at[j]),
            message(slot, 3, dpy.at[j], dhl.at[j]),
        ]

    setup = [
        message(PERM_SLOT, 0, perm.at[1], perm.at[BX + 1]),
        message(PERM_SLOT, 1, perm.at[BX], perm.at[0]),
        message(PRESS_SLOT, 0, press.at[1], press.at[BX + 1]),
        message(PRESS_SLOT, 1, press.at[BX], press.at[0]),
        message(PERM_SLOT, 2, ps, psr),
        message(PERM_SLOT, 3, ps, psl),
        message(CONC_SLOT, 0, conc.at[1], conc.at[BX + 1]),
        message(CONC_SLOT, 1, conc.at[BX], conc.at[0]),
    ]

    zero_tile = jnp.zeros((8, LANES), F32)
    lane = iota((NZ, LANES), 1)
    first_lane = lane == 0
    last_lane = lane == LANES - 1
    level = iota((NZ, LANES), 0)

    arrived("conc", "rock", "por", "adj")
    for x in range(BX):
        kind = rock[x]
        bits = [(kind // (1 << b)) % 2 == 1 for b in range(3)]

        def look_up(row, s):
            level_values = [sorp[row, i, s] for i in range(ROCKS)]
            for b in range(3):
                level_values = [
                    jnp.where(bits[b], level_values[2 * i + 1], level_values[2 * i])
                    for i in range(len(level_values) // 2)
                ]
            return level_values[0]

        hole = por[x]
        for s in range(SPEC):
            lang = look_up(0, s)
            cap = look_up(1, s)
            base = 1.0 + lang * conc[x + 1, s]
            base = base * base
            inv = base / (hole * (base + cap * lang))
            ia[x, s] = inv
            first = adj[x, s] * inv
            w[0, x + 1, s] = first
            wacc[x + 1, s] = first
    for s in range(SPEC):
        packed = zero_tile
        for x in range(BX):
            packed = pack_row(w[0, x + 1, s], x, packed)
        py[0, s] = packed
        pw[s] = packed
    arrived("perm", "press")
    for i, field in enumerate((perm, press)):
        packed = zero_tile
        for x in range(BX):
            packed = pack_row(field[x + 1], x, packed)
        ps[i] = packed
    for s in range(SPEC):
        packed = zero_tile
        for x in range(BX):
            packed = pack_row(conc[x + 1, s], x, packed)
        ps[2 + s] = packed

    pl.semaphore_wait(barrier, 4)
    for copy in setup[:6]:
        copy.start()
    for s in range(SPEC):
        for copy in transport_messages(0, s):
            copy.start()
    for copy in setup[6:]:
        copy.start()

    arrived("up", "sto")
    for copy in setup[:6]:
        copy.wait_recv()
    even = iota((8, LANES), 1) % 2 == 0
    perm_edge = align(psl[0], psr[0])
    perm_edge = jnp.where(even, jnp.where(gy == 0, 0.0, perm_edge), jnp.where(gy == ny - 1, 0.0, perm_edge))
    press_edge = align(psl[1], psr[1])
    for x in range(BX):
        own = perm[x + 1]
        head = press[x + 1]
        perm_n = perm[x] if x > 0 else jnp.where(gx == 0, 0.0, perm[x])
        perm_s = perm[x + 2] if x < BX - 1 else jnp.where(gx == nx - 1, 0.0, perm[x + 2])
        edge = unpack_row(perm_edge, x)
        perm_w = jnp.where(first_lane, edge, pltpu.roll(own, 1, 1))
        perm_e = jnp.where(last_lane, edge, pltpu.roll(own, LANES - 1, 1))
        perm_b = jnp.where(level == 0, 0.0, pltpu.roll(own, 1, 0))
        perm_a = jnp.where(level == NZ - 1, 0.0, pltpu.roll(own, NZ - 1, 0))
        edge = unpack_row(press_edge, x)
        drops = [
            head - press[x],
            head - press[x + 2],
            head - jnp.where(first_lane, edge, pltpu.roll(head, 1, 1)),
            head - jnp.where(last_lane, edge, pltpu.roll(head, LANES - 1, 1)),
            head - pltpu.roll(head, 1, 0),
            head - pltpu.roll(head, NZ - 1, 0),
        ]
        trans = []
        for i, near in enumerate((perm_n, perm_s, perm_w, perm_e, perm_b, perm_a)):
            inv = 1.0 / (own + near)
            trans.append(2.0 * own * near * inv)
            share = near * inv
            kk[i, x] = 2.0 * share * share * drops[i]
        total = sto[x]
        for item in trans:
            total = total + item
        inv_diag = 1.0 / total
        centre = None
        for i in range(4):
            up_here = (up[x, i] == 1) if i in (1, 3) else (up[x, i] != 1)
            push = jnp.where(up_here, STEP * trans[i] * jnp.abs(drops[i]), 0.0)
            coef[i, x] = push
            centre = push if centre is None else centre + push
        coef[4, x] = centre
        for i in range(6):
            ratio = trans[i] * inv_diag
            tau[i, x] = ratio
            if i < 4:
                ratio = STEP * ratio
                st[i, x] = jnp.where(drops[i] > 0, ratio, jnp.where(drops[i] < 0, -ratio, 0.0))

    def advance(t, s, last):
        for copy in transport_messages(t, s):
            copy.wait_recv()
        halo = align(hyl[t, s], hyr[t, s])

        @pl.when(t == 0)
        def _():
            hyw[s] = halo
            wacc[0, s] = w[t, 0, s]
            wacc[BX + 1, s] = w[t, BX + 1, s]

        @pl.when(t > 0)
        def _():
            hyw[s] = hyw[s] + halo
            wacc[0, s] = wacc[0, s] + w[t, 0, s]
            wacc[BX + 1, s] = wacc[BX + 1, s] + w[t, BX + 1, s]

        packed = zero_tile
        for x in range(BX):
            value = w[t, x + 1, s]
            edge = unpack_row(halo, x)
            west = jnp.where(first_lane, edge, pltpu.roll(value, 1, 1))
            east = jnp.where(last_lane, edge, pltpu.roll(value, LANES - 1, 1))
            moved = (
                adj[x, s]
                + (coef[0, x] * w[t, x, s] + coef[1, x] * w[t, x + 2, s])
                + (coef[2, x] * west + coef[3, x] * east)
                - coef[4, x] * value
            )
            adj[x, s] = moved
            if not last:
                after = moved * ia[x, s]
                w[t + 1, x + 1, s] = after
                wacc[x + 1, s] = wacc[x + 1, s] + after
                packed = pack_row(after, x, packed)
        if not last:
            py[t + 1, s] = packed
            pw[s] = pw[s] + packed
            for copy in transport_messages(t + 1, s):
                copy.start()

    @pl.loop(0, (SUB - 1) * SPEC)
    def _(i):
        advance(i // SPEC, i % SPEC, False)

    @pl.loop(0, SPEC)
    def _(s):
        advance(SUB - 1, s, True)

    writes = []
    for x in range(BX):
        copy = pltpu.make_async_copy(adj.at[x], out_h.at[:, :, x, :], in_sems.at[0, x])
        copy.start()
        writes.append(copy)

    for copy in setup[6:]:
        copy.wait_recv()
    flag_edge = zero_tile
    for x in range(BX):
        flag_edge = pack_row(jnp.where(first_lane, up[x, 2], up[x, 3]).astype(F32), x, flag_edge)
    flag_edge = pltpu.roll(flag_edge, LANES - 1, 1) == 1.0
    face_edge = zero_tile
    for s in range(SPEC):
        sum_halo = hyw[s]
        sum_own = pltpu.roll(pw[s], LANES - 1, 1)
        conc_halo = align(psl[2 + s], psr[2 + s])
        conc_own = pltpu.roll(ps[2 + s], LANES - 1, 1)
        low = jnp.where(even, conc_halo, conc_own)
        high = jnp.where(even, conc_own, conc_halo)
        rise = jnp.where(even, sum_own - sum_halo, sum_halo - sum_own)
        face_edge = face_edge + jnp.where(flag_edge, low, high) * rise

    def x_face(x):
        flag = (up[x, 0] if x < BX else up[x - 1, 1]) == 1
        total = None
        for s in range(SPEC):
            term = jnp.where(flag, conc[x, s], conc[x + 1, s]) * (wacc[x + 1, s] - wacc[x, s])
            total = term if total is None else total + term
        return total

    before = x_face(0)
    packed = zero_tile
    for x in range(BX):
        after = x_face(x + 1)
        flag = up[x, 3] == 1
        east = None
        for s in range(SPEC):
            here = conc[x + 1, s]
            mine = wacc[x + 1, s]
            term = jnp.where(flag, here, pltpu.roll(here, LANES - 1, 1)) * (pltpu.roll(mine, LANES - 1, 1) - mine)
            east = term if east is None else east + term
        edge = unpack_row(face_edge, x)
        west = jnp.where(first_lane, edge, pltpu.roll(east, 1, 1))
        east = jnp.where(last_lane, edge, east)
        faces = (before, after, west, east)
        start = None
        slope = None
        for i in range(4):
            one = st[i, x] * faces[i]
            two = jnp.abs(kk[i, x]) * faces[i]
            start = one if start is None else start + one
            slope = two if slope is None else slope + two
        grad[x] = STEP * slope
        d[0, x + 1] = start
        r[x] = start
        m[x] = start
        packed = pack_row(start, x, packed)
        before = after
    dpy[0] = packed
    for copy in cheb_messages(0):
        copy.start()

    def neighbours(j, x, halo):
        value = d[j, x + 1]
        edge = unpack_row(halo, x)
        return (
            d[j, x],
            d[j, x + 2],
            jnp.where(first_lane, edge, pltpu.roll(value, 1, 1)),
            jnp.where(last_lane, edge, pltpu.roll(value, LANES - 1, 1)),
            pltpu.roll(value, 1, 0),
            pltpu.roll(value, NZ - 1, 0),
        )

    rho = CONTRACT
    for j in range(CHEB - 1):
        rho_next = 1.0 / (2.0 / CONTRACT - rho)
        for copy in cheb_messages(j):
            copy.wait_recv()
        halo = align(dhl[j], dhr[j])
        packed = zero_tile
        for x in range(BX):
            value = d[j, x + 1]
            residue = r[x] - value
            for i, near in enumerate(neighbours(j, x, halo)):
                residue = residue + tau[i, x] * near
            r[x] = residue
            value = (rho_next * rho) * value + (2.0 * rho_next / CONTRACT) * residue
            total = m[x] + value
            m[x] = total
            if j == CHEB - 2:
                value = total
            d[j + 1, x + 1] = value
            packed = pack_row(value, x, packed)
        dpy[j + 1] = packed
        for copy in cheb_messages(j + 1):
            copy.start()
        rho = rho_next

    j = CHEB - 1
    for copy in cheb_messages(j):
        copy.wait_recv()
    halo = align(dhl[j], dhr[j])
    for x in range(BX):
        value = d[j, x + 1]
        total = grad[x]
        for i, near in enumerate(neighbours(j, x, halo)):
            total = total - kk[i, x] * (value - near)
        grad[x] = total
        copy = pltpu.make_async_copy(grad.at[x], grad_h.at[:, x, :], in_sems.at[1, x])
        copy.start()
        writes.append(copy)

    for copy in setup:
        copy.wait_send()
    for j in range(CHEB):
        for copy in cheb_messages(j):
            copy.wait_send()

    @pl.loop(0, SUB * SPEC)
    def _(i):
        for copy in transport_messages(i // SPEC, i % SPEC):
            copy.wait_send()

    for copy in writes:
        copy.wait()


def body(adjoint_in, conc, pressure, perm, porosity, storage, rock, upwind, sorption):
    def vmem(*shape, dtype=F32):
        return pltpu.VMEM(shape, dtype)

    row = (NZ, LANES)
    tile = (8, LANES)
    hbm = pl.BlockSpec(memory_space=pl.ANY)
    return tuple(pl.pallas_call(
        kernel,
        out_shape=(
            jax.ShapeDtypeStruct(adjoint_in.shape, F32),
            jax.ShapeDtypeStruct(pressure.shape, F32),
        ),
        in_specs=[hbm] * 8 + [pl.BlockSpec(memory_space=pltpu.SMEM)],
        out_specs=(hbm, hbm),
        scratch_shapes=[
            vmem(BX, SPEC, *row),
            vmem(BX + 2, SPEC, *row),
            vmem(BX + 2, *row),
            vmem(BX + 2, *row),
            vmem(BX, *row),
            vmem(BX, *row),
            vmem(BX, *row, dtype=jnp.int32),
            vmem(BX, 4, *row, dtype=jnp.int32),
            vmem(BX, SPEC, *row),
            vmem(SUB, BX + 2, SPEC, *row),
            vmem(BX + 2, SPEC, *row),
            vmem(SUB, SPEC, *tile),
            vmem(SUB, SPEC, *tile),
            vmem(SUB, SPEC, *tile),
            vmem(SPEC, *tile),
            vmem(SPEC, *tile),
            vmem(2 + SPEC, *tile),
            vmem(2 + SPEC, *tile),
            vmem(2 + SPEC, *tile),
            vmem(5, BX, *row),
            vmem(6, BX, *row),
            vmem(4, BX, *row),
            vmem(6, BX, *row),
            vmem(CHEB, BX + 2, *row),
            vmem(CHEB, *tile),
            vmem(CHEB, *tile),
            vmem(CHEB, *tile),
            vmem(BX, *row),
            vmem(BX, *row),
            vmem(BX, *row),
            pltpu.SemaphoreType.DMA((8, BX)),
            pltpu.SemaphoreType.DMA((SLOTS, 4)),
            pltpu.SemaphoreType.DMA((SLOTS, 4)),
        ],
        compiler_params=pltpu.CompilerParams(
            collective_id=0, has_side_effects=True, vmem_limit_bytes=48 * 2**20),
    )(adjoint_in, conc, pressure, perm, porosity, storage, rock, upwind, sorption))


def solution(mesh):
    in_specs = (
        P(None, None, "gx", "gy"),
        P(None, None, "gx", "gy"),
        P(None, "gx", "gy"),
        P(None, "gx", "gy"),
        P(None, "gx", "gy"),
        P(None, "gx", "gy"),
        P(None, "gx", "gy"),
        P(None, None, "gx", "gy"),
        P(),
    )
    out_specs = (P(None, None, "gx", "gy"), P(None, "gx", "gy"))
    return jax.shard_map(body, mesh=mesh, in_specs=in_specs, out_specs=out_specs, check_vma=False)
```

```python
import jax
import jax.numpy as jnp
from jax import lax
from jax.experimental import pallas as pl
from jax.experimental.pallas import tpu as pltpu
from jax.sharding import PartitionSpec as P

ROCKS = 8
SUB = 8
CHEB = 4
SPEC = 4
NZ = 48
BX = 8
LANES = 128
ZT = NZ // 8
STEP = 0.02
CONTRACT = 0.9
F32 = jnp.float32
MESH = pl.DeviceIdType.MESH

TIMES = (0, 1, 3, 5, 7)
ROUNDS = len(TIMES)

CHEB_SLOT = ROUNDS * SPEC
PERM_SLOT = CHEB_SLOT + 2
PRESS_SLOT = PERM_SLOT + 1
CONC_SLOT = PERM_SLOT + 2
COEF_SLOT = PERM_SLOT + 3
AREA_SLOT = PERM_SLOT + 4
TAU_SLOT = PERM_SLOT + 5
SLOTS = PERM_SLOT + 6


def iota(shape, dim):
    return lax.broadcasted_iota(jnp.int32, shape, dim)


def pack(rows):
    index = iota((8, LANES), 1) // 2
    packed = None
    for x, values in enumerate(rows):
        part = None
        for zt in range(ZT):
            t = x * ZT + zt
            turned = pltpu.roll(values[8 * zt:8 * zt + 8], 2 * t + 1, 1)
            part = turned if part is None else jnp.where(index >= t, turned, part)
        packed = part if packed is None else jnp.where(index >= x * ZT, part, packed)
    return packed


def pack_second(rows):
    lane = iota((8, LANES), 1)
    index = jnp.where(lane % 2 == 0, lane // 2, (lane + LANES - 3) % LANES // 2)
    packed = None
    for x, values in enumerate(rows):
        part = None
        for zt in range(ZT):
            t = x * ZT + zt
            turned = pltpu.roll(values[8 * zt:8 * zt + 8], 2 * t + 2, 1)
            part = turned if part is None else jnp.where(index >= t, turned, part)
        packed = part if packed is None else jnp.where(index >= x * ZT, part, packed)
    return packed


def unpack_row(packed, x):
    tiles = []
    for zt in range(ZT):
        t = x * ZT + zt
        tiles.append(pltpu.roll(packed, LANES - 2 * t, 1) if t else packed)
    return jnp.concatenate(tiles, axis=0)


def align(left, right):
    even = iota((8, LANES), 1) % 2 == 0
    return jnp.where(even, left, pltpu.roll(right, LANES - 2, 1))


def align_second(left, right):
    even = iota((8, LANES), 1) % 2 == 0
    return jnp.where(even, left, pltpu.roll(right, LANES - 4, 1))


def corners(north_west, north_east, south_west, south_east):
    even = iota((8, LANES), 1) % 2 == 0
    shift = 2 * ZT * (BX - 1)
    north = jnp.where(even, pltpu.roll(north_west, LANES - shift, 1), pltpu.roll(north_east, LANES - shift - 2, 1))
    south = jnp.where(even, pltpu.roll(south_west, shift, 1), pltpu.roll(south_east, shift - 2, 1))
    return north, south


def strip_sides(strip, second, own, north, south):
    lane = iota((8, LANES), 1)
    even = lane % 2 == 0
    row = 2 * ZT
    above = jnp.where((lane + 1) % LANES < row, north, pltpu.roll(strip, row, 1))
    edge = row * (BX - 1) - 1
    below = jnp.where((lane >= edge) & (lane < edge + row), south, pltpu.roll(strip, LANES - row, 1))
    return above, below, jnp.where(even, second, own), jnp.where(even, own, second)


def kernel(adj_h, conc_h, press_h, perm_h, por_h, sto_h, rock_h, up_h, sorp_h, out_h, grad_h,
           adj, conc, press, perm, por, sto, rock, up, ia, w, wacc, py, hyl, hyr, hyw,
           hc, ps, psl, psr, qs, ql, qr, ts, tl, tr, coef, tau, st, kk, d, dpy, dhl, dhr, dhc,
           m, r, grad, sorp, in_sems, send, recv):
    gx = lax.axis_index("gx")
    gy = lax.axis_index("gy")
    nx = lax.axis_size("gx")
    ny = lax.axis_size("gy")
    to = [
        {"gx": lax.rem(gx + nx - 1, nx), "gy": gy},
        {"gx": lax.rem(gx + 1, nx), "gy": gy},
        {"gx": gx, "gy": lax.rem(gy + ny - 1, ny)},
        {"gx": gx, "gy": lax.rem(gy + 1, ny)},
    ]
    to += [{"gx": a["gx"], "gy": b["gy"]} for a in to[:2] for b in to[2:]]

    loads = {}

    def load(i, name, src, dst):
        loads[name] = []
        for x in range(BX):
            copy = pltpu.make_async_copy(src(x), dst(x), in_sems.at[i, x])
            copy.start()
            loads[name].append(copy)

    def arrived(*names):
        for name in names:
            for copy in loads[name]:
                copy.wait()

    barrier = pltpu.get_barrier_semaphore()
    for target in to:
        pl.semaphore_signal(barrier, inc=1, device_id=target, device_id_type=MESH)
    table = pltpu.make_async_copy(sorp_h, sorp, in_sems.at[8, 0])
    table.start()
    load(0, "conc", lambda x: conc_h.at[:, :, x, :], lambda x: conc.at[x + 1])
    load(1, "rock", lambda x: rock_h.at[:, x, :], lambda x: rock.at[x])
    load(2, "por", lambda x: por_h.at[:, x, :], lambda x: por.at[x])
    load(3, "adj", lambda x: adj_h.at[:, :, x, :], lambda x: adj.at[x])
    load(4, "perm", lambda x: perm_h.at[:, x, :], lambda x: perm.at[x + 1])
    load(5, "press", lambda x: press_h.at[:, x, :], lambda x: press.at[x + 1])
    load(6, "up", lambda x: up_h.at[:, :, x, :], lambda x: up.at[x])
    load(7, "sto", lambda x: sto_h.at[:, x, :], lambda x: sto.at[x])

    def message(slot, way, src, dst):
        return pltpu.make_async_remote_copy(
            src_ref=src, dst_ref=dst, send_sem=send.at[slot, way], recv_sem=recv.at[slot, way],
            device_id=to[way], device_id_type=MESH)

    def row_messages(slot, field, wide):
        if wide:
            return [
                message(slot, 0, field(2, 2), field(BX + 2, 2)),
                message(slot, 1, field(BX, 2), field(0, 2)),
            ]
        return [
            message(slot, 0, field(2, 1), field(BX + 2, 1)),
            message(slot, 1, field(BX + 1, 1), field(1, 1)),
        ]

    def exchange(e, t, s, wide):
        slot = e * SPEC + s
        copies = row_messages(slot, lambda x, n: w.at[t, pl.ds(x, n), s], wide)
        if wide:
            copies += [
                message(slot, 2, py.at[e, s], hyr.at[e, s]),
                message(slot, 3, py.at[e, s], hyl.at[e, s]),
            ]
            copies += [message(slot, 4 + q, py.at[e, s, 0], hc.at[e, s, 3 - q]) for q in range(4)]
        else:
            copies += [
                message(slot, 2, py.at[e, s, 0], hyr.at[e, s, 0]),
                message(slot, 3, py.at[e, s, 0], hyl.at[e, s, 0]),
            ]
        return copies

    def cheb_exchange(e):
        slot = CHEB_SLOT + e
        copies = row_messages(slot, lambda x, n: d.at[2 * e, pl.ds(x, n)], True)
        copies += [
            message(slot, 2, dpy.at[e], dhr.at[e]),
            message(slot, 3, dpy.at[e], dhl.at[e]),
        ]
        copies += [message(slot, 4 + q, dpy.at[e, 0], dhc.at[e, 3 - q]) for q in range(4)]
        return copies

    def beside(slot, field):
        return [
            message(slot, 0, field.at[1], field.at[BX + 1]),
            message(slot, 1, field.at[BX], field.at[0]),
        ]

    second = beside(COEF_SLOT, coef) + beside(AREA_SLOT, ia) + [
        message(COEF_SLOT, 2, qs, qr),
        message(COEF_SLOT, 3, qs, ql),
    ]
    third = beside(TAU_SLOT, tau) + [
        message(TAU_SLOT, 2, ts, tr),
        message(TAU_SLOT, 3, ts, tl),
    ]
    setup = [
        message(PERM_SLOT, 0, perm.at[1], perm.at[BX + 1]),
        message(PERM_SLOT, 1, perm.at[BX], perm.at[0]),
        message(PRESS_SLOT, 0, press.at[1], press.at[BX + 1]),
        message(PRESS_SLOT, 1, press.at[BX], press.at[0]),
        message(PERM_SLOT, 2, ps, psr),
        message(PERM_SLOT, 3, ps, psl),
        message(CONC_SLOT, 0, conc.at[1], conc.at[BX + 1]),
        message(CONC_SLOT, 1, conc.at[BX], conc.at[0]),
    ]

    zero_tile = jnp.zeros((8, LANES), F32)
    lane = iota((NZ, LANES), 1)
    first_lane = lane == 0
    last_lane = lane == LANES - 1
    level = iota((NZ, LANES), 0)

    table.wait()
    arrived("conc", "rock", "por", "adj")
    for x in range(BX):
        kind = rock[x]
        bits = [(kind // (1 << b)) % 2 == 1 for b in range(3)]

        def look_up(row, s):
            level_values = [sorp[row, s, i] for i in range(ROCKS)]
            for b in range(3):
                level_values = [
                    jnp.where(bits[b], level_values[2 * i + 1], level_values[2 * i])
                    for i in range(len(level_values) // 2)
                ]
            return level_values[0]

        hole = por[x]
        for s in range(SPEC):
            lang = look_up(0, s)
            cap = look_up(1, s)
            base = 1.0 + lang * conc[x + 1, s]
            base = base * base
            inv = base / (hole * (base + cap * lang))
            ia[x + 1, s] = inv
            first = adj[x, s] * inv
            w[0, x + 2, s] = first
            wacc[x + 1, s] = first
    for s in range(SPEC):
        py[0, s, 0] = pack([w[0, x + 2, s] for x in range(BX)])
    arrived("perm", "press")
    ps[0] = pack([perm[x + 1] for x in range(BX)])
    ps[1] = pack([press[x + 1] for x in range(BX)])
    for s in range(SPEC):
        ps[2 + s] = pack([conc[x + 1, s] for x in range(BX)])

    pl.semaphore_wait(barrier, 8)
    for copy in setup[:6]:
        copy.start()
    for s in range(SPEC):
        for copy in exchange(0, 0, s, False):
            copy.start()
    for copy in setup[6:]:
        copy.start()

    arrived("up", "sto")
    for copy in setup[:6]:
        copy.wait_recv()
    even = iota((8, LANES), 1) % 2 == 0
    perm_edge = align(psl[0], psr[0])
    perm_edge = jnp.where(even, jnp.where(gy == 0, 0.0, perm_edge), jnp.where(gy == ny - 1, 0.0, perm_edge))
    press_edge = align(psl[1], psr[1])
    for x in range(BX):
        own = perm[x + 1]
        head = press[x + 1]
        perm_n = perm[x] if x > 0 else jnp.where(gx == 0, 0.0, perm[x])
        perm_s = perm[x + 2] if x < BX - 1 else jnp.where(gx == nx - 1, 0.0, perm[x + 2])
        edge = unpack_row(perm_edge, x)
        perm_w = jnp.where(first_lane, edge, pltpu.roll(own, 1, 1))
        perm_e = jnp.where(last_lane, edge, pltpu.roll(own, LANES - 1, 1))
        perm_b = jnp.where(level == 0, 0.0, pltpu.roll(own, 1, 0))
        perm_a = jnp.where(level == NZ - 1, 0.0, pltpu.roll(own, NZ - 1, 0))
        edge = unpack_row(press_edge, x)
        drops = [
            head - press[x],
            head - press[x + 2],
            head - jnp.where(first_lane, edge, pltpu.roll(head, 1, 1)),
            head - jnp.where(last_lane, edge, pltpu.roll(head, LANES - 1, 1)),
            head - pltpu.roll(head, 1, 0),
            head - pltpu.roll(head, NZ - 1, 0),
        ]
        trans = []
        for i, near in enumerate((perm_n, perm_s, perm_w, perm_e, perm_b, perm_a)):
            inv = 1.0 / (own + near)
            trans.append(2.0 * own * near * inv)
            share = near * inv
            kk[i, x] = 2.0 * share * share * drops[i]
        total = sto[x]
        for item in trans:
            total = total + item
        inv_diag = 1.0 / total
        centre = None
        for i in range(4):
            up_here = (up[x, i] == 1) if i in (1, 3) else (up[x, i] != 1)
            push = jnp.where(up_here, STEP * trans[i] * jnp.abs(drops[i]), 0.0)
            coef[x + 1, i] = push
            centre = push if centre is None else centre + push
        coef[x + 1, 4] = centre
        for i in range(6):
            ratio = trans[i] * inv_diag
            tau[x + 1, i] = ratio
            if i < 4:
                ratio = STEP * ratio
                st[i, x] = jnp.where(drops[i] > 0, ratio, jnp.where(drops[i] < 0, -ratio, 0.0))

    for i in range(4):
        qs[i] = pack([coef[x + 1, i] for x in range(BX)])
    for s in range(SPEC):
        qs[4 + s] = pack([ia[x + 1, s] for x in range(BX)])
    for copy in second:
        copy.start()

    def narrow(t, s, halo, e):
        fresh = []
        for x in range(BX):
            value = w[t, x + 2, s]
            edge = unpack_row(halo, x)
            west = jnp.where(first_lane, edge, pltpu.roll(value, 1, 1))
            east = jnp.where(last_lane, edge, pltpu.roll(value, LANES - 1, 1))
            moved = (
                adj[x, s]
                + (coef[x + 1, 0] * w[t, x + 1, s] + coef[x + 1, 1] * w[t, x + 3, s])
                + (coef[x + 1, 2] * west + coef[x + 1, 3] * east)
                - coef[x + 1, 4] * value
            )
            adj[x, s] = moved
            if e is not None:
                after = moved * ia[x + 1, s]
                w[t + 1, x + 2, s] = after
                wacc[x + 1, s] = wacc[x + 1, s] + after
                fresh.append(after)
        if e is not None:
            py[e, s, 0] = pack(fresh)
            py[e, s, 1] = pack_second(fresh)
            for copy in exchange(e, t + 1, s, True):
                copy.start()

    def wide(t, s, e):
        for copy in exchange(e, t, s, True):
            copy.wait_recv()
        strip = align(hyl[e, s, 0], hyr[e, s, 0])
        further = align_second(hyl[e, s, 1], hyr[e, s, 1])
        north, south = corners(hc[e, s, 0], hc[e, s, 1], hc[e, s, 2], hc[e, s, 3])
        sides = strip_sides(strip, further, pltpu.roll(py[e, s, 0], LANES - 1, 1), north, south)
        share = [align(ql[i], qr[i]) for i in range(4)]
        change = -(share[0] + share[1] + share[2] + share[3]) * strip
        for i in range(4):
            change = change + share[i] * sides[i]
        strip_next = strip + align(ql[4 + s], qr[4 + s]) * change
        hyw[s] = hyw[s] + (strip + strip_next)
        for x in range(-1, BX + 1):
            value = w[t, x + 2, s]
            edge = unpack_row(north, 0) if x < 0 else unpack_row(south, BX - 1) if x == BX else unpack_row(strip, x)
            west = jnp.where(first_lane, edge, pltpu.roll(value, 1, 1))
            east = jnp.where(last_lane, edge, pltpu.roll(value, LANES - 1, 1))
            change = (
                (coef[x + 1, 0] * w[t, x + 1, s] + coef[x + 1, 1] * w[t, x + 3, s])
                + (coef[x + 1, 2] * west + coef[x + 1, 3] * east)
                - coef[x + 1, 4] * value
            )
            if 0 <= x < BX:
                moved = adj[x, s] + change
                adj[x, s] = moved
                after = moved * ia[x + 1, s]
                wacc[x + 1, s] = wacc[x + 1, s] + after
            else:
                after = value + ia[x + 1, s] * change
                wacc[x + 1, s] = wacc[x + 1, s] + (value + after)
            w[t + 1, x + 2, s] = after
        return strip_next

    @pl.loop(0, SPEC)
    def _(s):
        for copy in exchange(0, 0, s, False):
            copy.wait_recv()
        halo = align(hyl[0, s, 0], hyr[0, s, 0])
        hyw[s] = halo
        wacc[0, s] = w[0, 1, s]
        wacc[BX + 1, s] = w[0, BX + 2, s]
        narrow(0, s, halo, 1)

    ts_rows = range(BX)
    for i in range(6):
        ts[i] = pack([tau[x + 1, i] for x in ts_rows])
    for copy in third:
        copy.start()
    for copy in second:
        copy.wait_recv()

    @pl.loop(0, (ROUNDS - 2) * SPEC)
    def _(i):
        e = i // SPEC + 1
        s = i % SPEC
        t = 2 * e - 1
        narrow(t + 1, s, wide(t, s, e), e + 1)

    @pl.loop(0, SPEC)
    def _(s):
        e = ROUNDS - 1
        t = SUB - 1
        for copy in exchange(e, t, s, True):
            copy.wait_recv()
        halo = align(hyl[e, s, 0], hyr[e, s, 0])
        hyw[s] = hyw[s] + halo
        wacc[0, s] = wacc[0, s] + w[t, 1, s]
        wacc[BX + 1, s] = wacc[BX + 1, s] + w[t, BX + 2, s]
        narrow(t, s, halo, None)

    writes = []
    for x in range(BX):
        copy = pltpu.make_async_copy(adj.at[x], out_h.at[:, :, x, :], in_sems.at[0, x])
        copy.start()
        writes.append(copy)

    for copy in setup[6:]:
        copy.wait_recv()
    flag_edge = pack([jnp.where(first_lane, up[x, 2], up[x, 3]).astype(F32) for x in range(BX)])
    flag_edge = pltpu.roll(flag_edge, LANES - 1, 1) == 1.0
    face_edge = zero_tile
    for s in range(SPEC):
        sum_halo = hyw[s]
        sum_own = pltpu.roll(pack([wacc[x + 1, s] for x in range(BX)]), LANES - 1, 1)
        conc_halo = align(psl[2 + s], psr[2 + s])
        conc_own = pltpu.roll(ps[2 + s], LANES - 1, 1)
        low = jnp.where(even, conc_halo, conc_own)
        high = jnp.where(even, conc_own, conc_halo)
        rise = jnp.where(even, sum_own - sum_halo, sum_halo - sum_own)
        face_edge = face_edge + jnp.where(flag_edge, low, high) * rise

    def x_face(x):
        flag = (up[x, 0] if x < BX else up[x - 1, 1]) == 1
        total = None
        for s in range(SPEC):
            term = jnp.where(flag, conc[x, s], conc[x + 1, s]) * (wacc[x + 1, s] - wacc[x, s])
            total = term if total is None else total + term
        return total

    before = x_face(0)
    fresh = []
    for x in range(BX):
        after = x_face(x + 1)
        flag = up[x, 3] == 1
        east = None
        for s in range(SPEC):
            here = conc[x + 1, s]
            mine = wacc[x + 1, s]
            term = jnp.where(flag, here, pltpu.roll(here, LANES - 1, 1)) * (pltpu.roll(mine, LANES - 1, 1) - mine)
            east = term if east is None else east + term
        edge = unpack_row(face_edge, x)
        west = jnp.where(first_lane, edge, pltpu.roll(east, 1, 1))
        east = jnp.where(last_lane, edge, east)
        faces = (before, after, west, east)
        start = None
        slope = None
        for i in range(4):
            one = st[i, x] * faces[i]
            two = jnp.abs(kk[i, x]) * faces[i]
            start = one if start is None else start + one
            slope = two if slope is None else slope + two
        grad[x] = STEP * slope
        d[0, x + 2] = start
        r[x] = start
        fresh.append(start)
        before = after
    dpy[0, 0] = pack(fresh)
    dpy[0, 1] = pack_second(fresh)
    for copy in cheb_exchange(0):
        copy.start()

    for copy in third:
        copy.wait_recv()
    ratios = [align(tl[i], tr[i]) for i in range(6)]

    def row_sides(field, x, edge):
        value = field(x)
        return (
            field(x - 1),
            field(x + 1),
            jnp.where(first_lane, edge, pltpu.roll(value, 1, 1)),
            jnp.where(last_lane, edge, pltpu.roll(value, LANES - 1, 1)),
            pltpu.roll(value, 1, 0),
            pltpu.roll(value, NZ - 1, 0),
        )

    def sweep(j, x, edge, residue, mix):
        value = d[j, x + 2]
        residue = residue - value
        for i, near in enumerate(row_sides(lambda y: d[j, y + 2], x, edge)):
            residue = residue + tau[x + 1, i] * near
        return residue, mix[0] * value + mix[1] * residue

    mixes = []
    rho = CONTRACT
    for j in range(CHEB - 1):
        rho_next = 1.0 / (2.0 / CONTRACT - rho)
        mixes.append((rho_next * rho, 2.0 * rho_next / CONTRACT))
        rho = rho_next
    back = 1.0 / mixes[1][1]

    def wide_sweep(j, strip_before):
        e = j // 2
        mix = mixes[j]
        for copy in cheb_exchange(e):
            copy.wait_recv()
        strip = align(dhl[e, 0], dhr[e, 0])
        further = align_second(dhl[e, 1], dhr[e, 1])
        north, south = corners(dhc[e, 0], dhc[e, 1], dhc[e, 2], dhc[e, 3])
        sides = strip_sides(strip, further, pltpu.roll(dpy[e, 0], LANES - 1, 1), north, south)
        floor = iota((8, LANES), 0)
        lower = pltpu.roll(strip, 1, 0)
        lower = jnp.where(floor == 0, pltpu.roll(lower, 2, 1), lower)
        upper = pltpu.roll(strip, 7, 0)
        upper = jnp.where(floor == 7, pltpu.roll(upper, LANES - 2, 1), upper)
        residue = strip if j == 0 else back * (strip - mixes[1][0] * strip_before)
        residue = residue - strip
        for i, near in enumerate(sides + (lower, upper)):
            residue = residue + ratios[i] * near
        strip_next = mix[0] * strip + mix[1] * residue
        for x in range(-1, BX + 1):
            edge = unpack_row(north, 0) if x < 0 else unpack_row(south, BX - 1) if x == BX else unpack_row(strip, x)
            if 0 <= x < BX:
                start = r[x]
            elif j == 0:
                start = d[j, x + 2]
            else:
                start = back * (d[j, x + 2] - mixes[1][0] * d[1, x + 2])
            residue, value = sweep(j, x, edge, start, mix)
            if 0 <= x < BX and j == 0:
                r[x] = residue
            d[j + 1, x + 2] = value
        return strip, strip_next

    strips = wide_sweep(0, None)
    fresh = []
    for x in range(BX):
        residue, value = sweep(1, x, unpack_row(strips[1], x), r[x], mixes[1])
        r[x] = residue
        d[2, x + 2] = value
        fresh.append(value)
    dpy[1, 0] = pack(fresh)
    dpy[1, 1] = pack_second(fresh)
    for copy in cheb_exchange(1):
        copy.start()
    strips += wide_sweep(2, strips[1])

    halo = (strips[0] + strips[1]) + (strips[2] + strips[3])
    for x in range(-1, BX + 1):
        m[x + 1] = (d[0, x + 2] + d[1, x + 2]) + (d[2, x + 2] + d[3, x + 2])
    for x in range(BX):
        value = m[x + 1]
        total = grad[x]
        for i, near in enumerate(row_sides(lambda y: m[y + 1], x, unpack_row(halo, x))):
            total = total - kk[i, x] * (value - near)
        grad[x] = total
        copy = pltpu.make_async_copy(grad.at[x], grad_h.at[:, x, :], in_sems.at[1, x])
        copy.start()
        writes.append(copy)

    for copy in setup + second + third:
        copy.wait_send()
    for e in range(2):
        for copy in cheb_exchange(e):
            copy.wait_send()

    @pl.loop(0, SPEC)
    def _(s):
        for copy in exchange(0, 0, s, False):
            copy.wait_send()

    @pl.loop(SPEC, ROUNDS * SPEC)
    def _(i):
        e = i // SPEC
        for copy in exchange(e, 2 * e - 1, i % SPEC, True):
            copy.wait_send()

    for copy in writes:
        copy.wait()


def body(adjoint_in, conc, pressure, perm, porosity, storage, rock, upwind, sorption):
    def vmem(*shape, dtype=F32):
        return pltpu.VMEM(shape, dtype)

    row = (NZ, LANES)
    tile = (8, LANES)
    hbm = pl.BlockSpec(memory_space=pltpu.HBM)
    return tuple(pl.pallas_call(
        kernel,
        out_shape=(
            jax.ShapeDtypeStruct(adjoint_in.shape, F32),
            jax.ShapeDtypeStruct(pressure.shape, F32),
        ),
        in_specs=[hbm] * 8 + [hbm],
        out_specs=(hbm, hbm),
        scratch_shapes=[
            vmem(BX, SPEC, *row),
            vmem(BX + 2, SPEC, *row),
            vmem(BX + 2, *row),
            vmem(BX + 2, *row),
            vmem(BX, *row),
            vmem(BX, *row),
            vmem(BX, *row, dtype=jnp.int32),
            vmem(BX, 4, *row, dtype=jnp.int32),
            vmem(BX + 2, SPEC, *row),
            vmem(SUB, BX + 4, SPEC, *row),
            vmem(BX + 2, SPEC, *row),
            vmem(ROUNDS, SPEC, 2, *tile),
            vmem(ROUNDS, SPEC, 2, *tile),
            vmem(ROUNDS, SPEC, 2, *tile),
            vmem(SPEC, *tile),
            vmem(ROUNDS, SPEC, 4, *tile),
            vmem(2 + SPEC, *tile),
            vmem(2 + SPEC, *tile),
            vmem(2 + SPEC, *tile),
            vmem(4 + SPEC, *tile),
            vmem(4 + SPEC, *tile),
            vmem(4 + SPEC, *tile),
            vmem(6, *tile),
            vmem(6, *tile),
            vmem(6, *tile),
            vmem(BX + 2, 5, *row),
            vmem(BX + 2, 6, *row),
            vmem(4, BX, *row),
            vmem(6, BX, *row),
            vmem(CHEB, BX + 4, *row),
            vmem(2, 2, *tile),
            vmem(2, 2, *tile),
            vmem(2, 2, *tile),
            vmem(2, 4, *tile),
            vmem(BX + 2, *row),
            vmem(BX, *row),
            vmem(BX, *row),
            pltpu.SMEM((2, SPEC, ROCKS), F32),
            pltpu.SemaphoreType.DMA((9, BX)),
            pltpu.SemaphoreType.DMA((SLOTS, 8)),
            pltpu.SemaphoreType.DMA((SLOTS, 8)),
        ],
        compiler_params=pltpu.CompilerParams(
            collective_id=0, has_side_effects=True, vmem_limit_bytes=63 * 2**20),
    )(adjoint_in, conc, pressure, perm, porosity, storage, rock, upwind, jnp.transpose(sorption, (0, 2, 1))))


def solution(mesh):
    in_specs = (
        P(None, None, "gx", "gy"),
        P(None, None, "gx", "gy"),
        P(None, "gx", "gy"),
        P(None, "gx", "gy"),
        P(None, "gx", "gy"),
        P(None, "gx", "gy"),
        P(None, "gx", "gy"),
        P(None, None, "gx", "gy"),
        P(),
    )
    out_specs = (P(None, None, "gx", "gy"), P(None, "gx", "gy"))
    return jax.shard_map(body, mesh=mesh, in_specs=in_specs, out_specs=out_specs, check_vma=False)
```

```python
import jax
import jax.numpy as jnp
from jax import lax
from jax.experimental import pallas as pl
from jax.experimental.pallas import tpu as pltpu
from jax.sharding import PartitionSpec as P

ROCKS = 8
SUB = 8
CHEB = 4
SPEC = 4
NZ = 48
BX = 8
LANES = 128
ZT = NZ // 8
STEP = 0.02
CONTRACT = 0.9
F32 = jnp.float32
MESH = pl.DeviceIdType.MESH

ROUNDS = SUB // 2

CHEB_SLOT = ROUNDS * SPEC
PERM_SLOT = CHEB_SLOT + 2
PRESS_SLOT = PERM_SLOT + 1
CONC_SLOT = PERM_SLOT + 2
FLAG_SLOT = PERM_SLOT + 3
TAU_SLOT = PERM_SLOT + 4
AREA_SLOT = PERM_SLOT + 5
SLOTS = AREA_SLOT + SPEC


def iota(shape, dim):
    return lax.broadcasted_iota(jnp.int32, shape, dim)


HALF = BX // 2
ROW_LANES = 4 * ZT


def pack_tile(values, t, packed):
    u = t % (HALF * ZT)
    if u == 0:
        return values
    index = (iota((8, LANES), 1) + 2) % LANES // 4
    return jnp.where(index >= u, pltpu.roll(values, 4 * u, 1), packed)


def pack_row(values, x, packed):
    part = packed[x // HALF]
    for zt in range(ZT):
        part = pack_tile(values[8 * zt:8 * zt + 8], x * ZT + zt, part)
    return (part, packed[1]) if x < HALF else (packed[0], part)


def unpack_row(packed, x):
    part = packed[x // HALF]
    tiles = []
    for zt in range(ZT):
        u = (x % HALF) * ZT + zt
        tiles.append(pltpu.roll(part, LANES - 4 * u, 1) if u else part)
    return jnp.concatenate(tiles, axis=0)


def from_left():
    return iota((8, LANES), 1) % 4 == 0


def align(left, right):
    return tuple(
        jnp.where(from_left(), pltpu.roll(left[h], 1, 1), pltpu.roll(right[h], LANES - 1, 1)) for h in range(2))


def align_second(left, right):
    return tuple(
        jnp.where(from_left(), pltpu.roll(left[h], 2, 1), pltpu.roll(right[h], LANES - 2, 1)) for h in range(2))


def corners(tiles):
    shift = ROW_LANES * (HALF - 1)
    north = jnp.where(
        from_left(), pltpu.roll(tiles[0], LANES - shift + 1, 1), pltpu.roll(tiles[1], LANES - shift - 1, 1))
    south = jnp.where(from_left(), pltpu.roll(tiles[2], shift + 1, 1), pltpu.roll(tiles[3], shift - 1, 1))
    return (north, None), (None, south)


def strip_sides(strip, second, own, north, south):
    lane = iota((8, LANES), 1)
    shift = ROW_LANES * (HALF - 1)
    top = (lane + 1) % LANES < ROW_LANES
    bottom = (lane >= shift - 1) & (lane < shift - 1 + ROW_LANES)
    above = (
        jnp.where(top, north[0], pltpu.roll(strip[0], ROW_LANES, 1)),
        jnp.where(top, pltpu.roll(strip[0], LANES - shift, 1), pltpu.roll(strip[1], ROW_LANES, 1)),
    )
    below = (
        jnp.where(bottom, pltpu.roll(strip[1], shift, 1), pltpu.roll(strip[0], LANES - ROW_LANES, 1)),
        jnp.where(bottom, south[1], pltpu.roll(strip[1], LANES - ROW_LANES, 1)),
    )
    west = tuple(jnp.where(from_left(), second[h], own[h]) for h in range(2))
    east = tuple(jnp.where(from_left(), own[h], second[h]) for h in range(2))
    return above, below, west, east


def kernel(adj_h, conc_h, press_h, perm_h, por_h, sto_h, rock_h, up_h, sorp_h, out_h, grad_h,
           adj, conc, press, perm, por, sto, rock, up, ia, w, wacc, py, hyl, hyr, hyw,
           hc, ps, psl, psr, cs, cl, cr, vs, vl, vr, fs, fl, fr, qs, hp, ts, tl, tr,
           coef, trans, tau, st, kk, d, dpy, dhl, dhr, dhc,
           m, r, grad, sorp, in_sems, send, recv):
    gx = lax.axis_index("gx")
    gy = lax.axis_index("gy")
    nx = lax.axis_size("gx")
    ny = lax.axis_size("gy")
    to = [
        {"gx": lax.rem(gx + nx - 1, nx), "gy": gy},
        {"gx": lax.rem(gx + 1, nx), "gy": gy},
        {"gx": gx, "gy": lax.rem(gy + ny - 1, ny)},
        {"gx": gx, "gy": lax.rem(gy + 1, ny)},
    ]
    to += [{"gx": a["gx"], "gy": b["gy"]} for a in to[:2] for b in to[2:]]

    loads = {}

    def load(i, name, src, dst):
        loads[name] = []
        for x in range(BX):
            copy = pltpu.make_async_copy(src(x), dst(x), in_sems.at[i, x])
            copy.start()
            loads[name].append(copy)

    def arrived(*names):
        for name in names:
            for copy in loads[name]:
                copy.wait()

    barrier = pltpu.get_barrier_semaphore()
    for target in to:
        pl.semaphore_signal(barrier, inc=1, device_id=target, device_id_type=MESH)
    table = pltpu.make_async_copy(sorp_h, sorp, in_sems.at[8, 0])
    table.start()
    load(0, "conc", lambda x: conc_h.at[:, :, x, :], lambda x: conc.at[x + 1])
    load(1, "rock", lambda x: rock_h.at[:, x, :], lambda x: rock.at[x])
    load(2, "por", lambda x: por_h.at[:, x, :], lambda x: por.at[x])
    load(3, "adj", lambda x: adj_h.at[:, :, x, :], lambda x: adj.at[x])
    load(4, "perm", lambda x: perm_h.at[:, x, :], lambda x: perm.at[x + 2])
    load(5, "press", lambda x: press_h.at[:, x, :], lambda x: press.at[x + 2])
    load(6, "up", lambda x: up_h.at[:, :, x, :], lambda x: up.at[x + 1])
    load(7, "sto", lambda x: sto_h.at[:, x, :], lambda x: sto.at[x])

    def message(slot, way, src, dst):
        return pltpu.make_async_remote_copy(
            src_ref=src, dst_ref=dst, send_sem=send.at[slot, way], recv_sem=recv.at[slot, way],
            device_id=to[way], device_id_type=MESH)

    def row_messages(slot, field):
        return [
            message(slot, 0, field(2), field(BX + 2)),
            message(slot, 1, field(BX), field(0)),
        ]

    def corner_messages(slot, own, there):
        return [message(slot, 4 + q, own(q // 2), there(3 - q)) for q in range(4)]

    def exchange(e, t, s):
        slot = e * SPEC + s
        copies = row_messages(slot, lambda x: w.at[t, pl.ds(x, 2), s])
        copies += columns(slot, py.at[e, s], hyl.at[e, s], hyr.at[e, s])
        return copies + corner_messages(slot, lambda h: py.at[e, s, h], lambda q: hc.at[e, s, q])

    def cheb_exchange(e):
        slot = CHEB_SLOT + e
        copies = row_messages(slot, lambda x: d.at[2 * e, pl.ds(x, 2)])
        copies += columns(slot, dpy.at[e], dhl.at[e], dhr.at[e])
        return copies + corner_messages(slot, lambda h: dpy.at[e, h], lambda q: dhc.at[e, q])

    def beside(slot, field):
        return [
            message(slot, 0, field.at[1], field.at[BX + 1]),
            message(slot, 1, field.at[BX], field.at[0]),
        ]

    def columns(slot, own, left, right):
        return [message(slot, 2, own, right), message(slot, 3, own, left)]

    press_rows = row_messages(PRESS_SLOT, lambda x: press.at[pl.ds(x, 2)])
    press_rows += corner_messages(PRESS_SLOT, lambda h: ps.at[1, h], lambda q: hp.at[1, q])
    perm_rows = row_messages(PERM_SLOT, lambda x: perm.at[pl.ds(x, 2)])
    perm_rows += corner_messages(PERM_SLOT, lambda h: ps.at[0, h], lambda q: hp.at[0, q])
    head_columns = columns(PERM_SLOT, ps, psl, psr)
    flag_rows = beside(FLAG_SLOT, up)
    flag_columns = columns(FLAG_SLOT, fs, fl, fr)
    conc_rows = beside(CONC_SLOT, conc)
    conc_columns = columns(CONC_SLOT, cs, cl, cr)
    area_rows = [
        [
            message(AREA_SLOT + s, 0, ia.at[1, s], ia.at[BX + 1, s]),
            message(AREA_SLOT + s, 1, ia.at[BX, s], ia.at[0, s]),
        ]
        for s in range(SPEC)
    ]
    area_columns = columns(AREA_SLOT, vs, vl, vr)
    tau_rows = beside(TAU_SLOT, tau)
    tau_columns = columns(TAU_SLOT, ts, tl, tr)

    def start(*groups):
        for group in groups:
            for copy in group:
                copy.start()

    def received(*groups):
        for group in groups:
            for copy in group:
                copy.wait_recv()

    def pack(rows):
        packed = (None, None)
        for x in range(BX):
            packed = pack_row(rows(x), x, packed)
        return packed

    def put(ref, *index, packed):
        for h in range(2):
            ref[(*index, h)] = packed[h]

    def get(ref, *index):
        return ref[(*index, 0)], ref[(*index, 1)]

    lane = iota((NZ, LANES), 1)
    first_lane = lane == 0
    last_lane = lane == LANES - 1
    level = iota((NZ, LANES), 0)

    table.wait()
    arrived("conc", "rock", "por", "adj")
    packs = [(None, None)] * SPEC
    area_packs = [(None, None)] * SPEC
    for x in range(BX):
        kind = rock[x]
        bits = [(kind // (1 << b)) % 2 == 1 for b in range(3)]

        def look_up(row, s):
            level_values = [sorp[row, s, i] for i in range(ROCKS)]
            for b in range(3):
                level_values = [
                    jnp.where(bits[b], level_values[2 * i + 1], level_values[2 * i])
                    for i in range(len(level_values) // 2)
                ]
            return level_values[0]

        hole = por[x]
        for s in range(SPEC):
            lang = look_up(0, s)
            cap = look_up(1, s)
            base = 1.0 + lang * conc[x + 1, s]
            base = base * base
            inv = base / (hole * (base + cap * lang))
            ia[x + 1, s] = inv
            first = adj[x, s] * inv
            w[0, x + 2, s] = first
            packs[s] = pack_row(first, x, packs[s])
            area_packs[s] = pack_row(inv, x, area_packs[s])
    for s in range(SPEC):
        put(py, 0, s, packed=packs[s])
        put(vs, s, packed=area_packs[s])
    nothing = jnp.zeros((NZ, LANES), F32)
    for x in range(BX + 2):
        for s in range(SPEC):
            wacc[x, s] = nothing
    for s in range(SPEC):
        put(hyw, s, packed=(nothing[:8], nothing[:8]))
    arrived("perm", "press", "up")
    put(ps, 0, packed=pack(lambda x: perm[x + 2]))
    put(ps, 1, packed=pack(lambda x: press[x + 2]))
    for i in range(4):
        put(fs, i, packed=pack(lambda x: up[x + 1, i].astype(F32)))

    pl.semaphore_wait(barrier, 8)
    start(perm_rows, press_rows, head_columns, flag_columns, flag_rows, area_columns)
    for s in range(SPEC):
        start(exchange(0, 0, s), area_rows[s])
    start(conc_rows)
    for s in range(SPEC):
        put(cs, s, packed=pack(lambda x: conc[x + 1, s]))
    start(conc_columns)

    received(perm_rows, press_rows, head_columns, flag_rows, flag_columns)

    def inside(pair, outside):
        return tuple(
            None if item is None else jnp.where(
                from_left(),
                jnp.where((gy == 0) | outside, 0.0, item),
                jnp.where((gy == ny - 1) | outside, 0.0, item),
            ) for item in pair)

    top_edge = gx == 0
    bottom_edge = gx == nx - 1
    perm_beside = align(get(psl, 0), get(psr, 0))
    press_beside = align(get(psl, 1), get(psr, 1))
    perm_edge = inside(perm_beside, False)
    perm_north, perm_south = corners([hp[0, q] for q in range(4)])
    perm_north = inside(perm_north, top_edge)
    perm_south = inside(perm_south, bottom_edge)
    press_north, press_south = corners([hp[1, q] for q in range(4)])

    def face(own, near, drop, flag, i):
        share = near / (own + near)
        item = 2.0 * own * share
        up_here = (flag == 1) if i in (1, 3) else (flag != 1)
        return share, item, jnp.where(up_here, STEP * item * jnp.abs(drop), 0.0)

    for x in range(-1, BX + 1):
        own = perm[x + 2]
        head = press[x + 2]
        perm_n = jnp.where(top_edge, 0.0, perm[x + 1]) if x == 0 else perm[x + 1]
        perm_s = jnp.where(bottom_edge, 0.0, perm[x + 3]) if x == BX - 1 else perm[x + 3]
        if x < 0:
            edge, head_edge = unpack_row(perm_north, 0), unpack_row(press_north, 0)
        elif x == BX:
            edge, head_edge = unpack_row(perm_south, BX - 1), unpack_row(press_south, BX - 1)
        else:
            edge, head_edge = unpack_row(perm_edge, x), unpack_row(press_beside, x)
        perm_w = jnp.where(first_lane, edge, pltpu.roll(own, 1, 1))
        perm_e = jnp.where(last_lane, edge, pltpu.roll(own, LANES - 1, 1))
        drops = (
            head - press[x + 1],
            head - press[x + 3],
            head - jnp.where(first_lane, head_edge, pltpu.roll(head, 1, 1)),
            head - jnp.where(last_lane, head_edge, pltpu.roll(head, LANES - 1, 1)),
        )
        centre = None
        for i, near in enumerate((perm_n, perm_s, perm_w, perm_e)):
            drop = drops[i]
            share, item, push = face(own, near, drop, up[x + 1, i], i)
            if 0 <= x < BX:
                trans[i, x] = item
                kk[i, x] = 2.0 * share * share * drop
                st[i, x] = STEP * jnp.where(drop > 0, item, jnp.where(drop < 0, -item, 0.0))
            coef[x + 1, i] = push
            centre = push if centre is None else centre + push
        coef[x + 1, 4] = centre

    perm_sides = strip_sides(
        perm_beside, align_second(get(psl, 0), get(psr, 0)), get(ps, 0), perm_north, perm_south)
    press_sides = strip_sides(
        press_beside, align_second(get(psl, 1), get(psr, 1)), get(ps, 1), press_north, press_south)
    for i in range(4):
        flag = align(get(fl, i), get(fr, i))
        put(qs, i, packed=tuple(
            face(perm_beside[h], perm_sides[i][h], press_beside[h] - press_sides[i][h], flag[h], i)[2]
            for h in range(2)))

    def repeat(t, s, first, last, edge, keep, store):
        above = w[t, first + 1, s]
        value = w[t, first + 2, s]
        for x in range(first, last):
            below = w[t, x + 3, s]
            beside_row = edge(x)
            west = jnp.where(first_lane, beside_row, pltpu.roll(value, 1, 1))
            east = jnp.where(last_lane, beside_row, pltpu.roll(value, LANES - 1, 1))
            change = (
                (coef[x + 1, 0] * above + coef[x + 1, 1] * below)
                + (coef[x + 1, 2] * west + coef[x + 1, 3] * east)
                - coef[x + 1, 4] * value
            )
            after = value + ia[x + 1, s] * change
            if store:
                w[t + 1, x + 2, s] = after
            keep(x, value, after)
            above, value = value, below

    def narrow(t, s, halo, e):
        packed = [(None, None)]

        def keep(x, value, after):
            packed[0] = pack_row(after, x, packed[0])

        repeat(t, s, 0, BX, lambda x: unpack_row(halo, x), keep, True)
        put(py, e, s, packed=packed[0])
        start(exchange(e, t + 1, s))

    def wide(t, s, e, store):
        received(exchange(e, t, s))
        strip = align(get(hyl, e, s), get(hyr, e, s))
        further = align_second(get(hyl, e, s), get(hyr, e, s))
        north, south = corners([hc[e, s, q] for q in range(4)])
        sides = strip_sides(strip, further, get(py, e, s), north, south)
        shares = [get(qs, i) for i in range(4)]
        scale = align(get(vl, s), get(vr, s))
        beyond = []
        for h in range(2):
            change = None
            for i in range(4):
                term = shares[i][h] * (sides[i][h] - strip[h])
                change = term if change is None else change + term
            after = strip[h] + scale[h] * change
            hyw[s, h] = hyw[s, h] + (strip[h] + after)
            beyond.append(after)

        def edge(x):
            return unpack_row(north, 0) if x < 0 else unpack_row(south, BX - 1) if x == BX else unpack_row(strip, x)

        def keep(x, value, after):
            wacc[x + 1, s] = wacc[x + 1, s] + (value + after)

        repeat(t, s, -1, BX + 1, edge, keep, store)
        return beyond

    received(area_columns)
    for s in range(SPEC):
        received(area_rows[s])
        narrow(1, s, wide(0, s, 0, True), 1)

    arrived("sto")
    packs = [(None, None)] * 6
    for x in range(BX):
        own = perm[x + 2]
        head = press[x + 2]
        items = [trans[i, x] for i in range(4)]
        for i, turn, end in ((4, 1, 0), (5, NZ - 1, NZ - 1)):
            near = jnp.where(level == end, 0.0, pltpu.roll(own, turn, 0))
            share = near / (own + near)
            items.append(2.0 * own * share)
            kk[i, x] = 2.0 * share * share * (head - pltpu.roll(head, turn, 0))
        total = sto[x]
        for item in items:
            total = total + item
        inv_diag = 1.0 / total
        for i in range(6):
            ratio = items[i] * inv_diag
            tau[x + 1, i] = ratio
            packs[i] = pack_row(ratio, x, packs[i])
            if i < 4:
                st[i, x] = st[i, x] * inv_diag
    for i in range(6):
        put(ts, i, packed=packs[i])
    start(tau_rows, tau_columns)

    @pl.loop(SPEC, (ROUNDS - 1) * SPEC)
    def _(i):
        e = i // SPEC
        s = i % SPEC
        narrow(2 * e + 1, s, wide(2 * e, s, e, True), e + 1)

    @pl.loop(0, SPEC)
    def _(s):
        wide(SUB - 2, s, ROUNDS - 1, False)

    received(conc_rows, conc_columns)
    writes = []

    conc_edge = [align(get(cl, s), get(cr, s)) for s in range(SPEC)]

    def x_face(x):
        flag = (up[x + 1, 0] if x < BX else up[x, 1]) == 1
        total = None
        for s in range(SPEC):
            term = jnp.where(flag, conc[x, s], conc[x + 1, s]) * (wacc[x + 1, s] - wacc[x, s])
            total = term if total is None else total + term
        return total

    before = x_face(0)
    packed = (None, None)
    for x in range(BX):
        after = x_face(x + 1)
        flag_west = up[x + 1, 2] == 1
        flag_east = up[x + 1, 3] == 1
        east = None
        for s in range(SPEC):
            here = conc[x + 1, s]
            mine = wacc[x + 1, s]
            here_edge = unpack_row(conc_edge[s], x)
            mine_edge = unpack_row(get(hyw, s), x)
            near = jnp.where(last_lane, here_edge, pltpu.roll(here, LANES - 1, 1))
            rise = jnp.where(last_lane, mine_edge, pltpu.roll(mine, LANES - 1, 1)) - mine
            term = jnp.where(flag_east, here, near) * rise
            east = term if east is None else east + term
            term = jnp.where(flag_west, here_edge, here) * (mine - mine_edge)
            west = term if s == 0 else west + term
        west = jnp.where(first_lane, west, pltpu.roll(east, 1, 1))
        faces = (before, after, west, east)
        start_row = None
        slope = None
        for i in range(4):
            one = st[i, x] * faces[i]
            two = jnp.abs(kk[i, x]) * faces[i]
            start_row = one if start_row is None else start_row + one
            slope = two if slope is None else slope + two
        grad[x] = STEP * slope
        d[0, x + 2] = start_row
        r[x] = start_row
        packed = pack_row(start_row, x, packed)
        before = after
    put(dpy, 0, packed=packed)
    start(cheb_exchange(0))

    for x in range(BX):
        for s in range(SPEC):
            value = wacc[x + 1, s]
            beside_row = unpack_row(get(hyw, s), x)
            west = jnp.where(first_lane, beside_row, pltpu.roll(value, 1, 1))
            east = jnp.where(last_lane, beside_row, pltpu.roll(value, LANES - 1, 1))
            adj[x, s] = adj[x, s] + (
                (coef[x + 1, 0] * wacc[x, s] + coef[x + 1, 1] * wacc[x + 2, s])
                + (coef[x + 1, 2] * west + coef[x + 1, 3] * east)
                - coef[x + 1, 4] * value
            )
        copy = pltpu.make_async_copy(adj.at[x], out_h.at[:, :, x, :], in_sems.at[0, x])
        copy.start()
        writes.append(copy)

    received(tau_rows, tau_columns)
    ratios = [align(get(tl, i), get(tr, i)) for i in range(6)]

    def row_sides(field, x, edge):
        value = field(x)
        return (
            field(x - 1),
            field(x + 1),
            jnp.where(first_lane, edge, pltpu.roll(value, 1, 1)),
            jnp.where(last_lane, edge, pltpu.roll(value, LANES - 1, 1)),
            pltpu.roll(value, 1, 0),
            pltpu.roll(value, NZ - 1, 0),
        )

    def sweep(j, x, edge, residue, mix):
        value = d[j, x + 2]
        residue = residue - value
        for i, near in enumerate(row_sides(lambda y: d[j, y + 2], x, edge)):
            residue = residue + tau[x + 1, i] * near
        return residue, mix[0] * value + mix[1] * residue

    mixes = []
    rho = CONTRACT
    for j in range(CHEB - 1):
        rho_next = 1.0 / (2.0 / CONTRACT - rho)
        mixes.append((rho_next * rho, 2.0 * rho_next / CONTRACT))
        rho = rho_next
    back = 1.0 / mixes[1][1]

    def wide_sweep(j, strip_before):
        e = j // 2
        mix = mixes[j]
        received(cheb_exchange(e))
        strip = align(get(dhl, e), get(dhr, e))
        further = align_second(get(dhl, e), get(dhr, e))
        north, south = corners([dhc[e, q] for q in range(4)])
        sides = strip_sides(strip, further, get(dpy, e), north, south)
        floor = iota((8, LANES), 0)
        beyond = []
        for h in range(2):
            lower = pltpu.roll(strip[h], 1, 0)
            lower = jnp.where(floor == 0, pltpu.roll(lower, 4, 1), lower)
            upper = pltpu.roll(strip[h], 7, 0)
            upper = jnp.where(floor == 7, pltpu.roll(upper, LANES - 4, 1), upper)
            residue = strip[h] if j == 0 else back * (strip[h] - mixes[1][0] * strip_before[h])
            residue = residue - strip[h]
            for i, near in enumerate([side[h] for side in sides] + [lower, upper]):
                residue = residue + ratios[i][h] * near
            beyond.append(mix[0] * strip[h] + mix[1] * residue)
        for x in range(-1, BX + 1):
            edge = unpack_row(north, 0) if x < 0 else unpack_row(south, BX - 1) if x == BX else unpack_row(strip, x)
            if 0 <= x < BX:
                begin = r[x]
            elif j == 0:
                begin = d[j, x + 2]
            else:
                begin = back * (d[j, x + 2] - mixes[1][0] * d[1, x + 2])
            residue, value = sweep(j, x, edge, begin, mix)
            if 0 <= x < BX and j == 0:
                r[x] = residue
            d[j + 1, x + 2] = value
        return strip, tuple(beyond)

    strips = wide_sweep(0, None)
    packed = (None, None)
    for x in range(BX):
        residue, value = sweep(1, x, unpack_row(strips[1], x), r[x], mixes[1])
        r[x] = residue
        d[2, x + 2] = value
        packed = pack_row(value, x, packed)
    put(dpy, 1, packed=packed)
    start(cheb_exchange(1))
    strips += wide_sweep(2, strips[1])

    halo = tuple((strips[0][h] + strips[1][h]) + (strips[2][h] + strips[3][h]) for h in range(2))
    for x in range(-1, BX + 1):
        m[x + 1] = (d[0, x + 2] + d[1, x + 2]) + (d[2, x + 2] + d[3, x + 2])
    for x in range(BX):
        value = m[x + 1]
        total = grad[x]
        for i, near in enumerate(row_sides(lambda y: m[y + 1], x, unpack_row(halo, x))):
            total = total - kk[i, x] * (value - near)
        grad[x] = total
        copy = pltpu.make_async_copy(grad.at[x], grad_h.at[:, x, :], in_sems.at[1, x])
        copy.start()
        writes.append(copy)

    for group in [perm_rows, press_rows, head_columns, conc_rows, conc_columns, area_columns,
                  flag_rows, flag_columns, tau_rows, tau_columns] + area_rows:
        for copy in group:
            copy.wait_send()
    for e in range(2):
        for copy in cheb_exchange(e):
            copy.wait_send()

    @pl.loop(0, ROUNDS * SPEC)
    def _(i):
        e = i // SPEC
        for copy in exchange(e, 2 * e, i % SPEC):
            copy.wait_send()

    for copy in writes:
        copy.wait()


def hand_over(adj, grad, adj_out, grad_out, adj_there, grad_there, sems):
    parts = [(adj.at[s], adj_there.at[s], adj_out.at[s]) for s in range(SPEC)] + [(grad, grad_there, grad_out)]
    inward = [pltpu.make_async_copy(a, b, sems.at[0, i]) for i, (a, b, c) in enumerate(parts)]
    outward = [pltpu.make_async_copy(b, c, sems.at[1, i]) for i, (a, b, c) in enumerate(parts)]
    for copy in inward:
        copy.start()
    for first, second in zip(inward, outward):
        first.wait()
        second.start()
    for copy in outward:
        copy.wait()


def body(adjoint_in, conc, pressure, perm, porosity, storage, rock, upwind, sorption):
    def vmem(*shape, dtype=F32):
        return pltpu.VMEM(shape, dtype)

    row = (NZ, LANES)
    tile = (8, LANES)
    hbm = pl.BlockSpec(memory_space=pltpu.HBM)
    adjoint_out, grad = pl.pallas_call(
        kernel,
        out_shape=(
            jax.ShapeDtypeStruct(adjoint_in.shape, F32),
            jax.ShapeDtypeStruct(pressure.shape, F32),
        ),
        in_specs=[hbm] * 8 + [hbm],
        out_specs=(hbm, hbm),
        scratch_shapes=[
            vmem(BX, SPEC, *row),
            vmem(BX + 2, SPEC, *row),
            vmem(BX + 4, *row),
            vmem(BX + 4, *row),
            vmem(BX, *row),
            vmem(BX, *row),
            vmem(BX, *row, dtype=jnp.int32),
            vmem(BX + 2, 4, *row, dtype=jnp.int32),
            vmem(BX + 2, SPEC, *row),
            vmem(SUB, BX + 4, SPEC, *row),
            vmem(BX + 2, SPEC, *row),
            vmem(ROUNDS, SPEC, 2, *tile),
            vmem(ROUNDS, SPEC, 2, *tile),
            vmem(ROUNDS, SPEC, 2, *tile),
            vmem(SPEC, 2, *tile),
            vmem(ROUNDS, SPEC, 4, *tile),
        ] + [vmem(2, 2, *tile)] * 3 + [
        ] + [vmem(SPEC, 2, *tile)] * 10 + [
            vmem(2, 4, *tile),
        ] + [vmem(6, 2, *tile)] * 3 + [
            vmem(BX + 2, 5, *row),
            vmem(4, BX, *row),
            vmem(BX + 2, 6, *row),
            vmem(4, BX, *row),
            vmem(6, BX, *row),
            vmem(CHEB, BX + 4, *row),
            vmem(2, 2, *tile),
            vmem(2, 2, *tile),
            vmem(2, 2, *tile),
            vmem(2, 4, *tile),
            vmem(BX + 2, *row),
            vmem(BX, *row),
            vmem(BX, *row),
            pltpu.SMEM((2, SPEC, ROCKS), F32),
            pltpu.SemaphoreType.DMA((9, BX)),
            pltpu.SemaphoreType.DMA((SLOTS, 8)),
            pltpu.SemaphoreType.DMA((SLOTS, 8)),
        ],
        compiler_params=pltpu.CompilerParams(
            collective_id=0, has_side_effects=True, vmem_limit_bytes=63 * 2**20),
    )(adjoint_in, conc, pressure, perm, porosity, storage, rock, upwind, jnp.transpose(sorption, (0, 2, 1)))
    return tuple(pl.pallas_call(
        hand_over,
        out_shape=(
            jax.ShapeDtypeStruct(adjoint_in.shape, F32),
            jax.ShapeDtypeStruct(pressure.shape, F32),
        ),
        in_specs=[hbm] * 2,
        out_specs=(hbm, hbm),
        scratch_shapes=[
            vmem(*adjoint_in.shape),
            vmem(*pressure.shape),
            pltpu.SemaphoreType.DMA((2, SPEC + 1)),
        ],
        compiler_params=pltpu.CompilerParams(vmem_limit_bytes=63 * 2**20),
    )(adjoint_out, grad))


def solution(mesh):
    in_specs = (
        P(None, None, "gx", "gy"),
        P(None, None, "gx", "gy"),
        P(None, "gx", "gy"),
        P(None, "gx", "gy"),
        P(None, "gx", "gy"),
        P(None, "gx", "gy"),
        P(None, "gx", "gy"),
        P(None, None, "gx", "gy"),
        P(),
    )
    out_specs = (P(None, None, "gx", "gy"), P(None, "gx", "gy"))
    return jax.shard_map(body, mesh=mesh, in_specs=in_specs, out_specs=out_specs, check_vma=False)
```

```python
import jax
import jax.numpy as jnp
from jax import lax
from jax.experimental import pallas as pl
from jax.experimental.pallas import tpu as pltpu
from jax.sharding import PartitionSpec as P

ROCKS = 8
SUB = 8
CHEB = 4
SPEC = 4
NZ = 48
BX = 8
LANES = 128
ZT = NZ // 8
STEP = 0.02
CONTRACT = 0.9
F32 = jnp.float32
MESH = pl.DeviceIdType.MESH

ROUNDS = SUB // 2

CHEB_SLOT = ROUNDS * SPEC
PERM_SLOT = CHEB_SLOT + 2
PRESS_SLOT = PERM_SLOT + 1
CONC_SLOT = PERM_SLOT + 2
FLAG_SLOT = PERM_SLOT + 3
TAU_SLOT = PERM_SLOT + 4
AREA_SLOT = PERM_SLOT + 5
SLOTS = AREA_SLOT + SPEC


def iota(shape, dim):
    return lax.broadcasted_iota(jnp.int32, shape, dim)


HALF = BX // 2
ROW_LANES = 4 * ZT


def pack_tile(values, t, packed):
    u = t % (HALF * ZT)
    if u == 0:
        return values
    index = (iota((8, LANES), 1) + 2) % LANES // 4
    return jnp.where(index >= u, pltpu.roll(values, 4 * u, 1), packed)


def pack_row(values, x, packed):
    part = packed[x // HALF]
    for zt in range(ZT):
        part = pack_tile(values[8 * zt:8 * zt + 8], x * ZT + zt, part)
    return (part, packed[1]) if x < HALF else (packed[0], part)


def unpack_row(packed, x):
    part = packed[x // HALF]
    tiles = []
    for zt in range(ZT):
        u = (x % HALF) * ZT + zt
        tiles.append(pltpu.roll(part, LANES - 4 * u, 1) if u else part)
    return jnp.concatenate(tiles, axis=0)


def from_left():
    return iota((8, LANES), 1) % 4 == 0


def align(left, right):
    return tuple(
        jnp.where(from_left(), pltpu.roll(left[h], 1, 1), pltpu.roll(right[h], LANES - 1, 1)) for h in range(2))


def align_second(left, right):
    return tuple(
        jnp.where(from_left(), pltpu.roll(left[h], 2, 1), pltpu.roll(right[h], LANES - 2, 1)) for h in range(2))


def corners(tiles):
    shift = ROW_LANES * (HALF - 1)
    north = jnp.where(
        from_left(), pltpu.roll(tiles[0], LANES - shift + 1, 1), pltpu.roll(tiles[1], LANES - shift - 1, 1))
    south = jnp.where(from_left(), pltpu.roll(tiles[2], shift + 1, 1), pltpu.roll(tiles[3], shift - 1, 1))
    return (north, None), (None, south)


def strip_sides(strip, second, own, north, south):
    lane = iota((8, LANES), 1)
    shift = ROW_LANES * (HALF - 1)
    top = (lane + 1) % LANES < ROW_LANES
    bottom = (lane >= shift - 1) & (lane < shift - 1 + ROW_LANES)
    above = (
        jnp.where(top, north[0], pltpu.roll(strip[0], ROW_LANES, 1)),
        jnp.where(top, pltpu.roll(strip[0], LANES - shift, 1), pltpu.roll(strip[1], ROW_LANES, 1)),
    )
    below = (
        jnp.where(bottom, pltpu.roll(strip[1], shift, 1), pltpu.roll(strip[0], LANES - ROW_LANES, 1)),
        jnp.where(bottom, south[1], pltpu.roll(strip[1], LANES - ROW_LANES, 1)),
    )
    west = tuple(jnp.where(from_left(), second[h], own[h]) for h in range(2))
    east = tuple(jnp.where(from_left(), own[h], second[h]) for h in range(2))
    return above, below, west, east


def kernel(adj_h, conc_h, press_h, perm_h, por_h, sto_h, rock_h, up_h, sorp_h, out_h, grad_h,
           adj, conc, press, perm, por, sto, rock, up, ia, w, wacc, py, hyl, hyr, hyw,
           hc, ps, psl, psr, cs, cl, cr, vs, vl, vr, fs, fl, fr, qs, hp, ts, tl, tr,
           coef, trans, tau, st, kk, d, dpy, dhl, dhr, dhc,
           m, r, grad, sorp, in_sems, send, recv):
    gx = lax.axis_index("gx")
    gy = lax.axis_index("gy")
    nx = lax.axis_size("gx")
    ny = lax.axis_size("gy")
    to = [
        {"gx": lax.rem(gx + nx - 1, nx), "gy": gy},
        {"gx": lax.rem(gx + 1, nx), "gy": gy},
        {"gx": gx, "gy": lax.rem(gy + ny - 1, ny)},
        {"gx": gx, "gy": lax.rem(gy + 1, ny)},
    ]
    to += [{"gx": a["gx"], "gy": b["gy"]} for a in to[:2] for b in to[2:]]

    loads = {}

    def load(i, name, src, dst):
        loads[name] = []
        for x in range(BX):
            copy = pltpu.make_async_copy(src(x), dst(x), in_sems.at[i, x])
            copy.start()
            loads[name].append(copy)

    def arrived(*names):
        for name in names:
            for copy in loads[name]:
                copy.wait()

    barrier = pltpu.get_barrier_semaphore()
    for target in to:
        pl.semaphore_signal(barrier, inc=1, device_id=target, device_id_type=MESH)
    table = pltpu.make_async_copy(sorp_h, sorp, in_sems.at[8, 0])
    table.start()
    load(0, "conc", lambda x: conc_h.at[:, :, x, :], lambda x: conc.at[x + 1])
    load(1, "rock", lambda x: rock_h.at[:, x, :], lambda x: rock.at[x])
    load(2, "por", lambda x: por_h.at[:, x, :], lambda x: por.at[x])
    load(3, "adj", lambda x: adj_h.at[:, :, x, :], lambda x: adj.at[x])
    load(4, "perm", lambda x: perm_h.at[:, x, :], lambda x: perm.at[x + 2])
    load(5, "press", lambda x: press_h.at[:, x, :], lambda x: press.at[x + 2])
    load(6, "up", lambda x: up_h.at[:, :, x, :], lambda x: up.at[x + 1])
    load(7, "sto", lambda x: sto_h.at[:, x, :], lambda x: sto.at[x])

    def message(slot, way, src, dst):
        return pltpu.make_async_remote_copy(
            src_ref=src, dst_ref=dst, send_sem=send.at[slot, way], recv_sem=recv.at[slot, way],
            device_id=to[way], device_id_type=MESH)

    def row_messages(slot, field):
        return [
            message(slot, 0, field(2), field(BX + 2)),
            message(slot, 1, field(BX), field(0)),
        ]

    def corner_messages(slot, own, there):
        return [message(slot, 4 + q, own(q // 2), there(3 - q)) for q in range(4)]

    def exchange(e, t, s):
        slot = e * SPEC + s
        copies = row_messages(slot, lambda x: w.at[t, pl.ds(x, 2), s])
        copies += columns(slot, py.at[e, s], hyl.at[e, s], hyr.at[e, s])
        return copies + corner_messages(slot, lambda h: py.at[e, s, h], lambda q: hc.at[e, s, q])

    def cheb_exchange(e):
        slot = CHEB_SLOT + e
        copies = row_messages(slot, lambda x: d.at[2 * e, pl.ds(x, 2)])
        copies += columns(slot, dpy.at[e], dhl.at[e], dhr.at[e])
        return copies + corner_messages(slot, lambda h: dpy.at[e, h], lambda q: dhc.at[e, q])

    def beside(slot, field):
        return [
            message(slot, 0, field.at[1], field.at[BX + 1]),
            message(slot, 1, field.at[BX], field.at[0]),
        ]

    def columns(slot, own, left, right):
        return [message(slot, 2, own, right), message(slot, 3, own, left)]

    press_rows = row_messages(PRESS_SLOT, lambda x: press.at[pl.ds(x, 2)])
    press_rows += corner_messages(PRESS_SLOT, lambda h: ps.at[1, h], lambda q: hp.at[1, q])
    perm_rows = row_messages(PERM_SLOT, lambda x: perm.at[pl.ds(x, 2)])
    perm_rows += corner_messages(PERM_SLOT, lambda h: ps.at[0, h], lambda q: hp.at[0, q])
    head_columns = columns(PERM_SLOT, ps, psl, psr)
    flag_rows = beside(FLAG_SLOT, up)
    flag_columns = columns(FLAG_SLOT, fs, fl, fr)
    conc_rows = beside(CONC_SLOT, conc)
    conc_columns = columns(CONC_SLOT, cs, cl, cr)
    area_rows = [
        [
            message(AREA_SLOT + s, 0, ia.at[1, s], ia.at[BX + 1, s]),
            message(AREA_SLOT + s, 1, ia.at[BX, s], ia.at[0, s]),
        ]
        for s in range(SPEC)
    ]
    area_columns = columns(AREA_SLOT, vs, vl, vr)
    tau_rows = beside(TAU_SLOT, tau)
    tau_columns = columns(TAU_SLOT, ts, tl, tr)

    def start(*groups):
        for group in groups:
            for copy in group:
                copy.start()

    def received(*groups):
        for group in groups:
            for copy in group:
                copy.wait_recv()

    def pack(rows):
        packed = (None, None)
        for x in range(BX):
            packed = pack_row(rows(x), x, packed)
        return packed

    def put(ref, *index, packed):
        for h in range(2):
            ref[(*index, h)] = packed[h]

    def get(ref, *index):
        return ref[(*index, 0)], ref[(*index, 1)]

    lane = iota((NZ, LANES), 1)
    first_lane = lane == 0
    last_lane = lane == LANES - 1
    level = iota((NZ, LANES), 0)

    table.wait()
    arrived("conc", "rock", "por", "adj")
    packs = [(None, None)] * SPEC
    area_packs = [(None, None)] * SPEC
    for x in range(BX):
        kind = rock[x]
        bits = [(kind // (1 << b)) % 2 == 1 for b in range(3)]

        def look_up(row, s):
            level_values = [sorp[row, s, i] for i in range(ROCKS)]
            for b in range(3):
                level_values = [
                    jnp.where(bits[b], level_values[2 * i + 1], level_values[2 * i])
                    for i in range(len(level_values) // 2)
                ]
            return level_values[0]

        hole = por[x]
        for s in range(SPEC):
            lang = look_up(0, s)
            cap = look_up(1, s)
            base = 1.0 + lang * conc[x + 1, s]
            base = base * base
            inv = base / (hole * (base + cap * lang))
            ia[x + 1, s] = inv
            first = adj[x, s] * inv
            w[0, x + 2, s] = first
            packs[s] = pack_row(first, x, packs[s])
            area_packs[s] = pack_row(inv, x, area_packs[s])
    for s in range(SPEC):
        put(py, 0, s, packed=packs[s])
        put(vs, s, packed=area_packs[s])
    nothing = jnp.zeros((NZ, LANES), F32)
    for x in range(BX + 2):
        for s in range(SPEC):
            wacc[x, s] = nothing
    for s in range(SPEC):
        put(hyw, s, packed=(nothing[:8], nothing[:8]))
    arrived("perm", "press", "up")
    put(ps, 0, packed=pack(lambda x: perm[x + 2]))
    put(ps, 1, packed=pack(lambda x: press[x + 2]))
    for i in range(4):
        put(fs, i, packed=pack(lambda x: up[x + 1, i].astype(F32)))

    pl.semaphore_wait(barrier, 8)
    start(perm_rows, press_rows, head_columns, flag_columns, flag_rows, area_columns)
    for s in range(SPEC):
        start(exchange(0, 0, s), area_rows[s])
    for s in range(SPEC):
        put(cs, s, packed=pack(lambda x: conc[x + 1, s]))

    received(perm_rows[:2], press_rows[:2], head_columns)

    def inside(pair, outside):
        return tuple(
            None if item is None else jnp.where(
                from_left(),
                jnp.where((gy == 0) | outside, 0.0, item),
                jnp.where((gy == ny - 1) | outside, 0.0, item),
            ) for item in pair)

    top_edge = gx == 0
    bottom_edge = gx == nx - 1
    perm_beside = align(get(psl, 0), get(psr, 0))
    press_beside = align(get(psl, 1), get(psr, 1))
    perm_edge = inside(perm_beside, False)
    def face(own, near, drop, flag, i):
        share = near / (own + near)
        item = 2.0 * own * share
        up_here = (flag == 1) if i in (1, 3) else (flag != 1)
        return share, item, jnp.where(up_here, STEP * item * jnp.abs(drop), 0.0)

    for x in (*range(BX), -1, BX):
        if x < 0:
            received(perm_rows[2:], press_rows[2:], flag_rows, flag_columns)
            perm_north, perm_south = corners([hp[0, q] for q in range(4)])
            perm_north = inside(perm_north, top_edge)
            perm_south = inside(perm_south, bottom_edge)
            press_north, press_south = corners([hp[1, q] for q in range(4)])
        own = perm[x + 2]
        head = press[x + 2]
        perm_n = jnp.where(top_edge, 0.0, perm[x + 1]) if x == 0 else perm[x + 1]
        perm_s = jnp.where(bottom_edge, 0.0, perm[x + 3]) if x == BX - 1 else perm[x + 3]
        if x < 0:
            edge, head_edge = unpack_row(perm_north, 0), unpack_row(press_north, 0)
        elif x == BX:
            edge, head_edge = unpack_row(perm_south, BX - 1), unpack_row(press_south, BX - 1)
        else:
            edge, head_edge = unpack_row(perm_edge, x), unpack_row(press_beside, x)
        perm_w = jnp.where(first_lane, edge, pltpu.roll(own, 1, 1))
        perm_e = jnp.where(last_lane, edge, pltpu.roll(own, LANES - 1, 1))
        drops = (
            head - press[x + 1],
            head - press[x + 3],
            head - jnp.where(first_lane, head_edge, pltpu.roll(head, 1, 1)),
            head - jnp.where(last_lane, head_edge, pltpu.roll(head, LANES - 1, 1)),
        )
        centre = None
        for i, near in enumerate((perm_n, perm_s, perm_w, perm_e)):
            drop = drops[i]
            share, item, push = face(own, near, drop, up[x + 1, i], i)
            if 0 <= x < BX:
                trans[i, x] = item
                kk[i, x] = 2.0 * share * share * drop
                st[i, x] = STEP * jnp.where(drop > 0, item, jnp.where(drop < 0, -item, 0.0))
            coef[x + 1, i] = push
            centre = push if centre is None else centre + push
        coef[x + 1, 4] = centre

    perm_sides = strip_sides(
        perm_beside, align_second(get(psl, 0), get(psr, 0)), get(ps, 0), perm_north, perm_south)
    press_sides = strip_sides(
        press_beside, align_second(get(psl, 1), get(psr, 1)), get(ps, 1), press_north, press_south)
    for i in range(4):
        flag = align(get(fl, i), get(fr, i))
        put(qs, i, packed=tuple(
            face(perm_beside[h], perm_sides[i][h], press_beside[h] - press_sides[i][h], flag[h], i)[2]
            for h in range(2)))

    def repeat(t, s, first, last, edge, keep, store):
        above = w[t, first + 1, s]
        value = w[t, first + 2, s]
        for x in range(first, last):
            below = w[t, x + 3, s]
            beside_row = edge(x)
            west = jnp.where(first_lane, beside_row, pltpu.roll(value, 1, 1))
            east = jnp.where(last_lane, beside_row, pltpu.roll(value, LANES - 1, 1))
            change = (
                (coef[x + 1, 0] * above + coef[x + 1, 1] * below)
                + (coef[x + 1, 2] * west + coef[x + 1, 3] * east)
                - coef[x + 1, 4] * value
            )
            after = value + ia[x + 1, s] * change
            if store:
                w[t + 1, x + 2, s] = after
            keep(x, value, after)
            above, value = value, below

    def narrow(t, s, halo, e):
        packed = [(None, None)]

        def keep(x, value, after):
            packed[0] = pack_row(after, x, packed[0])

        repeat(t, s, 0, BX, lambda x: unpack_row(halo, x), keep, True)
        put(py, e, s, packed=packed[0])
        start(exchange(e, t + 1, s))

    def wide(t, s, e, store):
        copies = exchange(e, t, s)
        received(copies[:4])
        strip = align(get(hyl, e, s), get(hyr, e, s))

        def keep(x, value, after):
            wacc[x + 1, s] = wacc[x + 1, s] + (value + after)

        repeat(t, s, 0, BX, lambda x: unpack_row(strip, x), keep, store)
        received(copies[4:])
        further = align_second(get(hyl, e, s), get(hyr, e, s))
        north, south = corners([hc[e, s, q] for q in range(4)])
        sides = strip_sides(strip, further, get(py, e, s), north, south)
        shares = [get(qs, i) for i in range(4)]
        scale = align(get(vl, s), get(vr, s))
        beyond = []
        for h in range(2):
            change = None
            for i in range(4):
                term = shares[i][h] * (sides[i][h] - strip[h])
                change = term if change is None else change + term
            after = strip[h] + scale[h] * change
            hyw[s, h] = hyw[s, h] + (strip[h] + after)
            beyond.append(after)
        repeat(t, s, -1, 0, lambda x: unpack_row(north, 0), keep, store)
        repeat(t, s, BX, BX + 1, lambda x: unpack_row(south, BX - 1), keep, store)
        return beyond

    received(area_columns)
    for s in range(SPEC):
        received(area_rows[s])
        narrow(1, s, wide(0, s, 0, True), 1)

    arrived("sto")
    packs = [(None, None)] * 6
    for x in range(BX):
        own = perm[x + 2]
        head = press[x + 2]
        items = [trans[i, x] for i in range(4)]
        for i, turn, end in ((4, 1, 0), (5, NZ - 1, NZ - 1)):
            near = jnp.where(level == end, 0.0, pltpu.roll(own, turn, 0))
            share = near / (own + near)
            items.append(2.0 * own * share)
            kk[i, x] = 2.0 * share * share * (head - pltpu.roll(head, turn, 0))
        total = sto[x]
        for item in items:
            total = total + item
        inv_diag = 1.0 / total
        for i in range(6):
            ratio = items[i] * inv_diag
            tau[x + 1, i] = ratio
            packs[i] = pack_row(ratio, x, packs[i])
            if i < 4:
                st[i, x] = st[i, x] * inv_diag
    for i in range(6):
        put(ts, i, packed=packs[i])
    start(tau_rows, tau_columns)

    @pl.loop(SPEC, (ROUNDS - 1) * SPEC)
    def _(i):
        e = i // SPEC
        s = i % SPEC
        narrow(2 * e + 1, s, wide(2 * e, s, e, True), e + 1)

        @pl.when(i == 2 * SPEC - 1)
        def _():
            start(conc_rows, conc_columns)

    @pl.loop(0, SPEC)
    def _(s):
        wide(SUB - 2, s, ROUNDS - 1, False)

    received(conc_rows, conc_columns)
    writes = []

    conc_edge = [align(get(cl, s), get(cr, s)) for s in range(SPEC)]

    def x_face(x):
        flag = (up[x + 1, 0] if x < BX else up[x, 1]) == 1
        total = None
        for s in range(SPEC):
            term = jnp.where(flag, conc[x, s], conc[x + 1, s]) * (wacc[x + 1, s] - wacc[x, s])
            total = term if total is None else total + term
        return total

    before = x_face(0)
    packed = (None, None)
    for x in range(BX):
        after = x_face(x + 1)
        flag_west = up[x + 1, 2] == 1
        flag_east = up[x + 1, 3] == 1
        east = None
        for s in range(SPEC):
            here = conc[x + 1, s]
            mine = wacc[x + 1, s]
            here_edge = unpack_row(conc_edge[s], x)
            mine_edge = unpack_row(get(hyw, s), x)
            near = jnp.where(last_lane, here_edge, pltpu.roll(here, LANES - 1, 1))
            rise = jnp.where(last_lane, mine_edge, pltpu.roll(mine, LANES - 1, 1)) - mine
            term = jnp.where(flag_east, here, near) * rise
            east = term if east is None else east + term
            term = jnp.where(flag_west, here_edge, here) * (mine - mine_edge)
            west = term if s == 0 else west + term
        west = jnp.where(first_lane, west, pltpu.roll(east, 1, 1))
        faces = (before, after, west, east)
        start_row = None
        slope = None
        for i in range(4):
            one = st[i, x] * faces[i]
            two = jnp.abs(kk[i, x]) * faces[i]
            start_row = one if start_row is None else start_row + one
            slope = two if slope is None else slope + two
        grad[x] = STEP * slope
        d[0, x + 2] = start_row
        r[x] = start_row
        packed = pack_row(start_row, x, packed)
        before = after
    put(dpy, 0, packed=packed)
    start(cheb_exchange(0))

    for x in range(BX):
        for s in range(SPEC):
            value = wacc[x + 1, s]
            beside_row = unpack_row(get(hyw, s), x)
            west = jnp.where(first_lane, beside_row, pltpu.roll(value, 1, 1))
            east = jnp.where(last_lane, beside_row, pltpu.roll(value, LANES - 1, 1))
            adj[x, s] = adj[x, s] + (
                (coef[x + 1, 0] * wacc[x, s] + coef[x + 1, 1] * wacc[x + 2, s])
                + (coef[x + 1, 2] * west + coef[x + 1, 3] * east)
                - coef[x + 1, 4] * value
            )
        copy = pltpu.make_async_copy(adj.at[x], out_h.at[:, :, x, :], in_sems.at[0, x])
        copy.start()
        writes.append(copy)

    received(tau_rows, tau_columns)
    ratios = [align(get(tl, i), get(tr, i)) for i in range(6)]

    def row_sides(field, x, edge):
        value = field(x)
        return (
            field(x - 1),
            field(x + 1),
            jnp.where(first_lane, edge, pltpu.roll(value, 1, 1)),
            jnp.where(last_lane, edge, pltpu.roll(value, LANES - 1, 1)),
            pltpu.roll(value, 1, 0),
            pltpu.roll(value, NZ - 1, 0),
        )

    def sweep(j, x, edge, residue, mix):
        value = d[j, x + 2]
        residue = residue - value
        for i, near in enumerate(row_sides(lambda y: d[j, y + 2], x, edge)):
            residue = residue + tau[x + 1, i] * near
        return residue, mix[0] * value + mix[1] * residue

    mixes = []
    rho = CONTRACT
    for j in range(CHEB - 1):
        rho_next = 1.0 / (2.0 / CONTRACT - rho)
        mixes.append((rho_next * rho, 2.0 * rho_next / CONTRACT))
        rho = rho_next
    back = 1.0 / mixes[1][1]

    def wide_sweep(j, strip_before):
        e = j // 2
        mix = mixes[j]
        copies = cheb_exchange(e)
        received(copies[:4])
        strip = align(get(dhl, e), get(dhr, e))
        for x in range(BX):
            residue, value = sweep(j, x, unpack_row(strip, x), r[x], mix)
            if j == 0:
                r[x] = residue
            d[j + 1, x + 2] = value
        received(copies[4:])
        further = align_second(get(dhl, e), get(dhr, e))
        north, south = corners([dhc[e, q] for q in range(4)])
        sides = strip_sides(strip, further, get(dpy, e), north, south)
        floor = iota((8, LANES), 0)
        beyond = []
        for h in range(2):
            lower = pltpu.roll(strip[h], 1, 0)
            lower = jnp.where(floor == 0, pltpu.roll(lower, 4, 1), lower)
            upper = pltpu.roll(strip[h], 7, 0)
            upper = jnp.where(floor == 7, pltpu.roll(upper, LANES - 4, 1), upper)
            residue = strip[h] if j == 0 else back * (strip[h] - mixes[1][0] * strip_before[h])
            residue = residue - strip[h]
            for i, near in enumerate([side[h] for side in sides] + [lower, upper]):
                residue = residue + ratios[i][h] * near
            beyond.append(mix[0] * strip[h] + mix[1] * residue)
        for x, edge in ((-1, unpack_row(north, 0)), (BX, unpack_row(south, BX - 1))):
            begin = d[j, x + 2]
            if j:
                begin = back * (begin - mixes[1][0] * d[1, x + 2])
            residue, value = sweep(j, x, edge, begin, mix)
            d[j + 1, x + 2] = value
        return strip, tuple(beyond)

    strips = wide_sweep(0, None)
    packed = (None, None)
    for x in range(BX):
        residue, value = sweep(1, x, unpack_row(strips[1], x), r[x], mixes[1])
        r[x] = residue
        d[2, x + 2] = value
        packed = pack_row(value, x, packed)
    put(dpy, 1, packed=packed)
    start(cheb_exchange(1))
    strips += wide_sweep(2, strips[1])

    halo = tuple((strips[0][h] + strips[1][h]) + (strips[2][h] + strips[3][h]) for h in range(2))
    for x in range(-1, BX + 1):
        m[x + 1] = (d[0, x + 2] + d[1, x + 2]) + (d[2, x + 2] + d[3, x + 2])
    for x in range(BX):
        value = m[x + 1]
        total = grad[x]
        for i, near in enumerate(row_sides(lambda y: m[y + 1], x, unpack_row(halo, x))):
            total = total - kk[i, x] * (value - near)
        grad[x] = total
        copy = pltpu.make_async_copy(grad.at[x], grad_h.at[:, x, :], in_sems.at[1, x])
        copy.start()
        writes.append(copy)

    for group in [perm_rows, press_rows, head_columns, conc_rows, conc_columns, area_columns,
                  flag_rows, flag_columns, tau_rows, tau_columns] + area_rows:
        for copy in group:
            copy.wait_send()
    for e in range(2):
        for copy in cheb_exchange(e):
            copy.wait_send()

    @pl.loop(0, ROUNDS * SPEC)
    def _(i):
        e = i // SPEC
        for copy in exchange(e, 2 * e, i % SPEC):
            copy.wait_send()

    for copy in writes:
        copy.wait()


def hand_over(adj, grad, adj_out, grad_out, adj_there, grad_there, sems):
    parts = [(adj.at[s], adj_there.at[s], adj_out.at[s]) for s in range(SPEC)] + [(grad, grad_there, grad_out)]
    inward = [pltpu.make_async_copy(a, b, sems.at[0, i]) for i, (a, b, c) in enumerate(parts)]
    outward = [pltpu.make_async_copy(b, c, sems.at[1, i]) for i, (a, b, c) in enumerate(parts)]
    for copy in inward:
        copy.start()
    for first, second in zip(inward, outward):
        first.wait()
        second.start()
    for copy in outward:
        copy.wait()


def body(adjoint_in, conc, pressure, perm, porosity, storage, rock, upwind, sorption):
    def vmem(*shape, dtype=F32):
        return pltpu.VMEM(shape, dtype)

    row = (NZ, LANES)
    tile = (8, LANES)
    hbm = pl.BlockSpec(memory_space=pltpu.HBM)
    adjoint_out, grad = pl.pallas_call(
        kernel,
        out_shape=(
            jax.ShapeDtypeStruct(adjoint_in.shape, F32),
            jax.ShapeDtypeStruct(pressure.shape, F32),
        ),
        in_specs=[hbm] * 8 + [hbm],
        out_specs=(hbm, hbm),
        scratch_shapes=[
            vmem(BX, SPEC, *row),
            vmem(BX + 2, SPEC, *row),
            vmem(BX + 4, *row),
            vmem(BX + 4, *row),
            vmem(BX, *row),
            vmem(BX, *row),
            vmem(BX, *row, dtype=jnp.int32),
            vmem(BX + 2, 4, *row, dtype=jnp.int32),
            vmem(BX + 2, SPEC, *row),
            vmem(SUB, BX + 4, SPEC, *row),
            vmem(BX + 2, SPEC, *row),
            vmem(ROUNDS, SPEC, 2, *tile),
            vmem(ROUNDS, SPEC, 2, *tile),
            vmem(ROUNDS, SPEC, 2, *tile),
            vmem(SPEC, 2, *tile),
            vmem(ROUNDS, SPEC, 4, *tile),
        ] + [vmem(2, 2, *tile)] * 3 + [
        ] + [vmem(SPEC, 2, *tile)] * 10 + [
            vmem(2, 4, *tile),
        ] + [vmem(6, 2, *tile)] * 3 + [
            vmem(BX + 2, 5, *row),
            vmem(4, BX, *row),
            vmem(BX + 2, 6, *row),
            vmem(4, BX, *row),
            vmem(6, BX, *row),
            vmem(CHEB, BX + 4, *row),
            vmem(2, 2, *tile),
            vmem(2, 2, *tile),
            vmem(2, 2, *tile),
            vmem(2, 4, *tile),
            vmem(BX + 2, *row),
            vmem(BX, *row),
            vmem(BX, *row),
            pltpu.SMEM((2, SPEC, ROCKS), F32),
            pltpu.SemaphoreType.DMA((9, BX)),
            pltpu.SemaphoreType.DMA((SLOTS, 8)),
            pltpu.SemaphoreType.DMA((SLOTS, 8)),
        ],
        compiler_params=pltpu.CompilerParams(
            collective_id=0, has_side_effects=True, vmem_limit_bytes=63 * 2**20),
    )(adjoint_in, conc, pressure, perm, porosity, storage, rock, upwind, jnp.transpose(sorption, (0, 2, 1)))
    return tuple(pl.pallas_call(
        hand_over,
        out_shape=(
            jax.ShapeDtypeStruct(adjoint_in.shape, F32),
            jax.ShapeDtypeStruct(pressure.shape, F32),
        ),
        in_specs=[hbm] * 2,
        out_specs=(hbm, hbm),
        scratch_shapes=[
            vmem(*adjoint_in.shape),
            vmem(*pressure.shape),
            pltpu.SemaphoreType.DMA((2, SPEC + 1)),
        ],
        compiler_params=pltpu.CompilerParams(vmem_limit_bytes=63 * 2**20),
    )(adjoint_out, grad))


def solution(mesh):
    in_specs = (
        P(None, None, "gx", "gy"),
        P(None, None, "gx", "gy"),
        P(None, "gx", "gy"),
        P(None, "gx", "gy"),
        P(None, "gx", "gy"),
        P(None, "gx", "gy"),
        P(None, "gx", "gy"),
        P(None, None, "gx", "gy"),
        P(),
    )
    out_specs = (P(None, None, "gx", "gy"), P(None, "gx", "gy"))
    return jax.shard_map(body, mesh=mesh, in_specs=in_specs, out_specs=out_specs, check_vma=False)
```

```python
import jax
import jax.numpy as jnp
from jax import lax
from jax.experimental import pallas as pl
from jax.experimental.pallas import tpu as pltpu
from jax.sharding import PartitionSpec as P

ROCKS = 8
SUB = 8
CHEB = 4
SPEC = 4
NZ = 48
BX = 8
LANES = 128
ZT = NZ // 8
STEP = 0.02
CONTRACT = 0.9
F32 = jnp.float32
MESH = pl.DeviceIdType.MESH

ROUNDS = SUB // 2

CHEB_SLOT = ROUNDS * SPEC
PERM_SLOT = CHEB_SLOT + 2
PRESS_SLOT = PERM_SLOT + 1
CONC_SLOT = PERM_SLOT + 2
FLAG_SLOT = PERM_SLOT + 3
TAU_SLOT = PERM_SLOT + 4
AREA_SLOT = PERM_SLOT + 5
SLOTS = AREA_SLOT + SPEC


def iota(shape, dim):
    return lax.broadcasted_iota(jnp.int32, shape, dim)


HALF = BX // 2
ROW_LANES = 4 * ZT
FLAG = (0, 3, 1, 2)


def pack_tile(values, t, packed):
    u = t % (HALF * ZT)
    if u == 0:
        return values
    index = (iota((8, LANES), 1) + 2) % LANES // 4
    return jnp.where(index >= u, pltpu.roll(values, 4 * u, 1), packed)


def pack_row(values, x, packed):
    part = packed[x // HALF]
    for zt in range(ZT):
        part = pack_tile(values[8 * zt:8 * zt + 8], x * ZT + zt, part)
    return (part, packed[1]) if x < HALF else (packed[0], part)


def unpack_row(packed, x):
    part = packed[x // HALF]
    tiles = []
    for zt in range(ZT):
        u = (x % HALF) * ZT + zt
        tiles.append(pltpu.roll(part, LANES - 4 * u, 1) if u else part)
    return jnp.concatenate(tiles, axis=0)


def from_left():
    return iota((8, LANES), 1) % 4 == 0


def align(left, right):
    return tuple(
        jnp.where(from_left(), pltpu.roll(left[h], 1, 1), pltpu.roll(right[h], LANES - 1, 1)) for h in range(2))


def align_second(left, right):
    return tuple(
        jnp.where(from_left(), pltpu.roll(left[h], 2, 1), pltpu.roll(right[h], LANES - 2, 1)) for h in range(2))


def corners(tiles):
    shift = ROW_LANES * (HALF - 1)
    north = jnp.where(
        from_left(), pltpu.roll(tiles[0], LANES - shift + 1, 1), pltpu.roll(tiles[1], LANES - shift - 1, 1))
    south = jnp.where(from_left(), pltpu.roll(tiles[2], shift + 1, 1), pltpu.roll(tiles[3], shift - 1, 1))
    return (north, None), (None, south)


def strip_sides(strip, second, own, north, south):
    lane = iota((8, LANES), 1)
    shift = ROW_LANES * (HALF - 1)
    top = (lane + 1) % LANES < ROW_LANES
    bottom = (lane >= shift - 1) & (lane < shift - 1 + ROW_LANES)
    above = (
        jnp.where(top, north[0], pltpu.roll(strip[0], ROW_LANES, 1)),
        jnp.where(top, pltpu.roll(strip[0], LANES - shift, 1), pltpu.roll(strip[1], ROW_LANES, 1)),
    )
    below = (
        jnp.where(bottom, pltpu.roll(strip[1], shift, 1), pltpu.roll(strip[0], LANES - ROW_LANES, 1)),
        jnp.where(bottom, south[1], pltpu.roll(strip[1], LANES - ROW_LANES, 1)),
    )
    west = tuple(jnp.where(from_left(), second[h], own[h]) for h in range(2))
    east = tuple(jnp.where(from_left(), own[h], second[h]) for h in range(2))
    return above, below, west, east


def kernel(adj_h, conc_h, press_h, perm_h, por_h, sto_h, rock_h, up_h, sorp_h, out_h, grad_h,
           adj, conc, press, perm, por, sto, rock, up, ia, w, wacc, py, hyl, hyr, hyw,
           hc, ps, psl, psr, cs, cl, cr, vs, vl, vr, fs, fl, fr, qs, hp, ts, tl, tr,
           coef, trans, tau, st, kk, d, dpy, dhl, dhr, dhc,
           m, r, grad, sorp, in_sems, send, recv):
    gx = lax.axis_index("gx")
    gy = lax.axis_index("gy")
    nx = lax.axis_size("gx")
    ny = lax.axis_size("gy")
    to = [
        {"gx": lax.rem(gx + nx - 1, nx), "gy": gy},
        {"gx": lax.rem(gx + 1, nx), "gy": gy},
        {"gx": gx, "gy": lax.rem(gy + ny - 1, ny)},
        {"gx": gx, "gy": lax.rem(gy + 1, ny)},
    ]
    to += [{"gx": a["gx"], "gy": b["gy"]} for a in to[:2] for b in to[2:]]

    loads = {}

    def load(i, name, src, dst):
        loads[name] = []
        for x in range(BX):
            copy = pltpu.make_async_copy(src(x), dst(x), in_sems.at[i, x])
            copy.start()
            loads[name].append(copy)

    def arrived(*names):
        for name in names:
            for copy in loads[name]:
                copy.wait()

    barrier = pltpu.get_barrier_semaphore()
    for target in to:
        pl.semaphore_signal(barrier, inc=1, device_id=target, device_id_type=MESH)
    table = pltpu.make_async_copy(sorp_h, sorp, in_sems.at[8, 0])
    table.start()
    load(0, "conc", lambda x: conc_h.at[:, :, x, :], lambda x: conc.at[x + 1])
    load(1, "rock", lambda x: rock_h.at[:, x, :], lambda x: rock.at[x])
    load(2, "por", lambda x: por_h.at[:, x, :], lambda x: por.at[x])
    load(3, "adj", lambda x: adj_h.at[:, :, x, :], lambda x: adj.at[x])
    load(4, "perm", lambda x: perm_h.at[:, x, :], lambda x: perm.at[x + 2])
    load(5, "press", lambda x: press_h.at[:, x, :], lambda x: press.at[x + 2])
    load(6, "up", lambda x: up_h.at[pl.ds(2, 2), :, x, :], lambda x: up.at[x + 1, pl.ds(1, 2)])
    load(9, "up north", lambda x: up_h.at[0, :, x, :], lambda x: up.at[x + 1, 0])
    load(10, "up south", lambda x: up_h.at[1, :, x, :], lambda x: up.at[x + 1, 3])
    load(7, "sto", lambda x: sto_h.at[:, x, :], lambda x: sto.at[x])

    def message(slot, way, src, dst):
        return pltpu.make_async_remote_copy(
            src_ref=src, dst_ref=dst, send_sem=send.at[slot, way], recv_sem=recv.at[slot, way],
            device_id=to[way], device_id_type=MESH)

    def row_messages(slot, field):
        return [
            message(slot, 0, field(2), field(BX + 2)),
            message(slot, 1, field(BX), field(0)),
        ]

    def corner_messages(slot, own, there):
        return [message(slot, 4 + q, own(q // 2), there(3 - q)) for q in range(4)]

    def exchange(e, t, s):
        slot = e * SPEC + s
        copies = row_messages(slot, lambda x: w.at[t, pl.ds(x, 2), s])
        copies += columns(slot, py.at[e, s], hyl.at[e, s], hyr.at[e, s])
        return copies + corner_messages(slot, lambda h: py.at[e, s, h], lambda q: hc.at[e, s, q])

    def cheb_exchange(e):
        slot = CHEB_SLOT + e
        copies = row_messages(slot, lambda x: d.at[2 * e, pl.ds(x, 2)])
        copies += columns(slot, dpy.at[e], dhl.at[e], dhr.at[e])
        return copies + corner_messages(slot, lambda h: dpy.at[e, h], lambda q: dhc.at[e, q])

    def beside(slot, field):
        return [
            message(slot, 0, field.at[1], field.at[BX + 1]),
            message(slot, 1, field.at[BX], field.at[0]),
        ]

    def columns(slot, own, left, right):
        return [message(slot, 2, own, right), message(slot, 3, own, left)]

    press_rows = row_messages(PRESS_SLOT, lambda x: press.at[pl.ds(x, 2)])
    press_rows += corner_messages(PRESS_SLOT, lambda h: ps.at[1, h], lambda q: hp.at[1, q])
    perm_rows = row_messages(PERM_SLOT, lambda x: perm.at[pl.ds(x, 2)])
    perm_rows += corner_messages(PERM_SLOT, lambda h: ps.at[0, h], lambda q: hp.at[0, q])
    head_columns = columns(PERM_SLOT, ps, psl, psr)
    flag_rows = [
        message(FLAG_SLOT, 0, up.at[1, pl.ds(1, 3)], up.at[BX + 1, pl.ds(1, 3)]),
        message(FLAG_SLOT, 1, up.at[BX, pl.ds(0, 3)], up.at[0, pl.ds(0, 3)]),
    ]
    flag_columns = columns(FLAG_SLOT, fs, fl, fr)
    conc_rows = beside(CONC_SLOT, conc)
    conc_columns = columns(CONC_SLOT, cs, cl, cr)
    area_rows = [
        [
            message(AREA_SLOT + s, 0, ia.at[1, s], ia.at[BX + 1, s]),
            message(AREA_SLOT + s, 1, ia.at[BX, s], ia.at[0, s]),
        ]
        for s in range(SPEC)
    ]
    area_columns = columns(AREA_SLOT, vs, vl, vr)
    tau_rows = beside(TAU_SLOT, tau)
    tau_columns = columns(TAU_SLOT, ts, tl, tr)

    def start(*groups):
        for group in groups:
            for copy in group:
                copy.start()

    def received(*groups):
        for group in groups:
            for copy in group:
                copy.wait_recv()

    def pack(rows):
        packed = (None, None)
        for x in range(BX):
            packed = pack_row(rows(x), x, packed)
        return packed

    def put(ref, *index, packed):
        for h in range(2):
            ref[(*index, h)] = packed[h]

    def get(ref, *index):
        return ref[(*index, 0)], ref[(*index, 1)]

    lane = iota((NZ, LANES), 1)
    first_lane = lane == 0
    last_lane = lane == LANES - 1
    level = iota((NZ, LANES), 0)

    table.wait()
    arrived("conc", "rock", "por", "adj")
    packs = [(None, None)] * SPEC
    area_packs = [(None, None)] * SPEC
    for x in range(BX):
        kind = rock[x]
        bits = [(kind // (1 << b)) % 2 == 1 for b in range(3)]

        def look_up(row, s):
            level_values = [sorp[row, s, i] for i in range(ROCKS)]
            for b in range(3):
                level_values = [
                    jnp.where(bits[b], level_values[2 * i + 1], level_values[2 * i])
                    for i in range(len(level_values) // 2)
                ]
            return level_values[0]

        hole = por[x]
        for s in range(SPEC):
            lang = look_up(0, s)
            cap = look_up(1, s)
            base = 1.0 + lang * conc[x + 1, s]
            base = base * base
            inv = base / (hole * (base + cap * lang))
            ia[x + 1, s] = inv
            first = adj[x, s] * inv
            w[0, x + 2, s] = first
            packs[s] = pack_row(first, x, packs[s])
            area_packs[s] = pack_row(inv, x, area_packs[s])
    for s in range(SPEC):
        put(py, 0, s, packed=packs[s])
        put(vs, s, packed=area_packs[s])
    nothing = jnp.zeros((NZ, LANES), F32)
    for x in range(BX + 2):
        for s in range(SPEC):
            wacc[x, s] = nothing
    for s in range(SPEC):
        put(hyw, s, packed=(nothing[:8], nothing[:8]))
    arrived("perm", "press", "up", "up north", "up south")
    put(ps, 0, packed=pack(lambda x: perm[x + 2]))
    put(ps, 1, packed=pack(lambda x: press[x + 2]))
    for i in range(4):
        put(fs, i, packed=pack(lambda x: up[x + 1, FLAG[i]].astype(F32)))

    pl.semaphore_wait(barrier, 8)
    start(perm_rows, press_rows, head_columns, flag_columns, flag_rows, area_columns)
    for s in range(SPEC):
        start(exchange(0, 0, s), area_rows[s])
    for s in range(SPEC):
        put(cs, s, packed=pack(lambda x: conc[x + 1, s]))

    received(perm_rows[:2], press_rows[:2], head_columns)

    def inside(pair, outside):
        return tuple(
            None if item is None else jnp.where(
                from_left(),
                jnp.where((gy == 0) | outside, 0.0, item),
                jnp.where((gy == ny - 1) | outside, 0.0, item),
            ) for item in pair)

    top_edge = gx == 0
    bottom_edge = gx == nx - 1
    perm_beside = align(get(psl, 0), get(psr, 0))
    press_beside = align(get(psl, 1), get(psr, 1))
    perm_edge = inside(perm_beside, False)
    def face(own, near, drop, flag, i):
        share = near / (own + near)
        item = 2.0 * own * share
        up_here = (flag == 1) if i in (1, 3) else (flag != 1)
        return share, item, jnp.where(up_here, STEP * item * jnp.abs(drop), 0.0)

    for x in (*range(BX), -1, BX):
        if x < 0:
            received(perm_rows[2:], press_rows[2:], flag_rows, flag_columns)
            perm_north, perm_south = corners([hp[0, q] for q in range(4)])
            perm_north = inside(perm_north, top_edge)
            perm_south = inside(perm_south, bottom_edge)
            press_north, press_south = corners([hp[1, q] for q in range(4)])
        own = perm[x + 2]
        head = press[x + 2]
        perm_n = jnp.where(top_edge, 0.0, perm[x + 1]) if x == 0 else perm[x + 1]
        perm_s = jnp.where(bottom_edge, 0.0, perm[x + 3]) if x == BX - 1 else perm[x + 3]
        if x < 0:
            edge, head_edge = unpack_row(perm_north, 0), unpack_row(press_north, 0)
        elif x == BX:
            edge, head_edge = unpack_row(perm_south, BX - 1), unpack_row(press_south, BX - 1)
        else:
            edge, head_edge = unpack_row(perm_edge, x), unpack_row(press_beside, x)
        perm_w = jnp.where(first_lane, edge, pltpu.roll(own, 1, 1))
        perm_e = jnp.where(last_lane, edge, pltpu.roll(own, LANES - 1, 1))
        drops = (
            head - press[x + 1],
            head - press[x + 3],
            head - jnp.where(first_lane, head_edge, pltpu.roll(head, 1, 1)),
            head - jnp.where(last_lane, head_edge, pltpu.roll(head, LANES - 1, 1)),
        )
        centre = None
        for i, near in enumerate((perm_n, perm_s, perm_w, perm_e)):
            drop = drops[i]
            flag = up[x + 1, FLAG[i]]
            if x < 0 and i == 1:
                flag = up[1, FLAG[0]]
            if x == BX and i == 0:
                flag = up[BX, FLAG[1]]
            share, item, push = face(own, near, drop, flag, i)
            if 0 <= x < BX:
                trans[i, x] = item
                kk[i, x] = 2.0 * share * share * drop
                st[i, x] = STEP * jnp.where(drop > 0, item, jnp.where(drop < 0, -item, 0.0))
            coef[x + 1, i] = push
            centre = push if centre is None else centre + push
        coef[x + 1, 4] = centre

    perm_sides = strip_sides(
        perm_beside, align_second(get(psl, 0), get(psr, 0)), get(ps, 0), perm_north, perm_south)
    press_sides = strip_sides(
        press_beside, align_second(get(psl, 1), get(psr, 1)), get(ps, 1), press_north, press_south)
    for i in range(4):
        flag = align(get(fl, i), get(fr, i))
        put(qs, i, packed=tuple(
            face(perm_beside[h], perm_sides[i][h], press_beside[h] - press_sides[i][h], flag[h], i)[2]
            for h in range(2)))

    def repeat(t, s, first, last, edge, keep, store):
        above = w[t, first + 1, s]
        value = w[t, first + 2, s]
        for x in range(first, last):
            below = w[t, x + 3, s]
            beside_row = edge(x)
            west = jnp.where(first_lane, beside_row, pltpu.roll(value, 1, 1))
            east = jnp.where(last_lane, beside_row, pltpu.roll(value, LANES - 1, 1))
            change = (
                (coef[x + 1, 0] * above + coef[x + 1, 1] * below)
                + (coef[x + 1, 2] * west + coef[x + 1, 3] * east)
                - coef[x + 1, 4] * value
            )
            after = value + ia[x + 1, s] * change
            if store:
                w[t + 1, x + 2, s] = after
            keep(x, value, after)
            above, value = value, below

    def narrow(t, s, halo, e):
        packed = [(None, None)]

        def keep(x, value, after):
            packed[0] = pack_row(after, x, packed[0])

        repeat(t, s, 0, BX, lambda x: unpack_row(halo, x), keep, True)
        put(py, e, s, packed=packed[0])
        start(exchange(e, t + 1, s))

    def wide(t, s, e, store):
        copies = exchange(e, t, s)
        received(copies[:4])
        strip = align(get(hyl, e, s), get(hyr, e, s))

        def keep(x, value, after):
            wacc[x + 1, s] = wacc[x + 1, s] + (value + after)

        repeat(t, s, 0, BX, lambda x: unpack_row(strip, x), keep, store)
        received(copies[4:])
        further = align_second(get(hyl, e, s), get(hyr, e, s))
        north, south = corners([hc[e, s, q] for q in range(4)])
        sides = strip_sides(strip, further, get(py, e, s), north, south)
        shares = [get(qs, i) for i in range(4)]
        scale = align(get(vl, s), get(vr, s))
        beyond = []
        for h in range(2):
            change = None
            for i in range(4):
                term = shares[i][h] * (sides[i][h] - strip[h])
                change = term if change is None else change + term
            after = strip[h] + scale[h] * change
            hyw[s, h] = hyw[s, h] + (strip[h] + after)
            beyond.append(after)
        repeat(t, s, -1, 0, lambda x: unpack_row(north, 0), keep, store)
        repeat(t, s, BX, BX + 1, lambda x: unpack_row(south, BX - 1), keep, store)
        return beyond

    received(area_columns)
    for s in range(SPEC):
        received(area_rows[s])
        narrow(1, s, wide(0, s, 0, True), 1)

    arrived("sto")
    packs = [(None, None)] * 6
    for x in range(BX):
        own = perm[x + 2]
        head = press[x + 2]
        items = [trans[i, x] for i in range(4)]
        for i, turn, end in ((4, 1, 0), (5, NZ - 1, NZ - 1)):
            near = jnp.where(level == end, 0.0, pltpu.roll(own, turn, 0))
            share = near / (own + near)
            items.append(2.0 * own * share)
            kk[i, x] = 2.0 * share * share * (head - pltpu.roll(head, turn, 0))
        total = sto[x]
        for item in items:
            total = total + item
        inv_diag = 1.0 / total
        for i in range(6):
            ratio = items[i] * inv_diag
            tau[x + 1, i] = ratio
            packs[i] = pack_row(ratio, x, packs[i])
            if i < 4:
                st[i, x] = st[i, x] * inv_diag
    for i in range(6):
        put(ts, i, packed=packs[i])
    start(tau_rows, tau_columns)

    @pl.loop(SPEC, (ROUNDS - 1) * SPEC)
    def _(i):
        e = i // SPEC
        s = i % SPEC
        narrow(2 * e + 1, s, wide(2 * e, s, e, True), e + 1)

        @pl.when(i == 2 * SPEC - 1)
        def _():
            start(conc_rows, conc_columns)

    @pl.loop(0, SPEC)
    def _(s):
        wide(SUB - 2, s, ROUNDS - 1, False)

    received(conc_rows, conc_columns)
    writes = []

    conc_edge = [align(get(cl, s), get(cr, s)) for s in range(SPEC)]

    def x_face(x):
        flag = (up[x + 1, FLAG[0]] if x < BX else up[x, FLAG[1]]) == 1
        total = None
        for s in range(SPEC):
            term = jnp.where(flag, conc[x, s], conc[x + 1, s]) * (wacc[x + 1, s] - wacc[x, s])
            total = term if total is None else total + term
        return total

    before = x_face(0)
    packed = (None, None)
    for x in range(BX):
        after = x_face(x + 1)
        flag_west = up[x + 1, FLAG[2]] == 1
        flag_east = up[x + 1, FLAG[3]] == 1
        east = None
        for s in range(SPEC):
            here = conc[x + 1, s]
            mine = wacc[x + 1, s]
            here_edge = unpack_row(conc_edge[s], x)
            mine_edge = unpack_row(get(hyw, s), x)
            near = jnp.where(last_lane, here_edge, pltpu.roll(here, LANES - 1, 1))
            rise = jnp.where(last_lane, mine_edge, pltpu.roll(mine, LANES - 1, 1)) - mine
            term = jnp.where(flag_east, here, near) * rise
            east = term if east is None else east + term
            term = jnp.where(flag_west, here_edge, here) * (mine - mine_edge)
            west = term if s == 0 else west + term
        west = jnp.where(first_lane, west, pltpu.roll(east, 1, 1))
        faces = (before, after, west, east)
        start_row = None
        slope = None
        for i in range(4):
            one = st[i, x] * faces[i]
            two = jnp.abs(kk[i, x]) * faces[i]
            start_row = one if start_row is None else start_row + one
            slope = two if slope is None else slope + two
        grad[x] = STEP * slope
        d[0, x + 2] = start_row
        r[x] = start_row
        packed = pack_row(start_row, x, packed)
        before = after
    put(dpy, 0, packed=packed)
    start(cheb_exchange(0))

    for x in range(BX):
        for s in range(SPEC):
            value = wacc[x + 1, s]
            beside_row = unpack_row(get(hyw, s), x)
            west = jnp.where(first_lane, beside_row, pltpu.roll(value, 1, 1))
            east = jnp.where(last_lane, beside_row, pltpu.roll(value, LANES - 1, 1))
            adj[x, s] = adj[x, s] + (
                (coef[x + 1, 0] * wacc[x, s] + coef[x + 1, 1] * wacc[x + 2, s])
                + (coef[x + 1, 2] * west + coef[x + 1, 3] * east)
                - coef[x + 1, 4] * value
            )
        copy = pltpu.make_async_copy(adj.at[x], out_h.at[:, :, x, :], in_sems.at[0, x])
        copy.start()
        writes.append(copy)

    received(tau_rows, tau_columns)
    ratios = [align(get(tl, i), get(tr, i)) for i in range(6)]

    def row_sides(field, x, edge):
        value = field(x)
        return (
            field(x - 1),
            field(x + 1),
            jnp.where(first_lane, edge, pltpu.roll(value, 1, 1)),
            jnp.where(last_lane, edge, pltpu.roll(value, LANES - 1, 1)),
            pltpu.roll(value, 1, 0),
            pltpu.roll(value, NZ - 1, 0),
        )

    def sweep(j, x, edge, residue, mix):
        value = d[j, x + 2]
        residue = residue - value
        for i, near in enumerate(row_sides(lambda y: d[j, y + 2], x, edge)):
            residue = residue + tau[x + 1, i] * near
        return residue, mix[0] * value + mix[1] * residue

    mixes = []
    rho = CONTRACT
    for j in range(CHEB - 1):
        rho_next = 1.0 / (2.0 / CONTRACT - rho)
        mixes.append((rho_next * rho, 2.0 * rho_next / CONTRACT))
        rho = rho_next
    back = 1.0 / mixes[1][1]

    def wide_sweep(j, strip_before):
        e = j // 2
        mix = mixes[j]
        copies = cheb_exchange(e)
        received(copies[:4])
        strip = align(get(dhl, e), get(dhr, e))
        for x in range(BX):
            residue, value = sweep(j, x, unpack_row(strip, x), r[x], mix)
            if j == 0:
                r[x] = residue
            d[j + 1, x + 2] = value
        received(copies[4:])
        further = align_second(get(dhl, e), get(dhr, e))
        north, south = corners([dhc[e, q] for q in range(4)])
        sides = strip_sides(strip, further, get(dpy, e), north, south)
        floor = iota((8, LANES), 0)
        beyond = []
        for h in range(2):
            lower = pltpu.roll(strip[h], 1, 0)
            lower = jnp.where(floor == 0, pltpu.roll(lower, 4, 1), lower)
            upper = pltpu.roll(strip[h], 7, 0)
            upper = jnp.where(floor == 7, pltpu.roll(upper, LANES - 4, 1), upper)
            residue = strip[h] if j == 0 else back * (strip[h] - mixes[1][0] * strip_before[h])
            residue = residue - strip[h]
            for i, near in enumerate([side[h] for side in sides] + [lower, upper]):
                residue = residue + ratios[i][h] * near
            beyond.append(mix[0] * strip[h] + mix[1] * residue)
        for x, edge in ((-1, unpack_row(north, 0)), (BX, unpack_row(south, BX - 1))):
            begin = d[j, x + 2]
            if j:
                begin = back * (begin - mixes[1][0] * d[1, x + 2])
            residue, value = sweep(j, x, edge, begin, mix)
            d[j + 1, x + 2] = value
        return strip, tuple(beyond)

    strips = wide_sweep(0, None)
    packed = (None, None)
    for x in range(BX):
        residue, value = sweep(1, x, unpack_row(strips[1], x), r[x], mixes[1])
        r[x] = residue
        d[2, x + 2] = value
        packed = pack_row(value, x, packed)
    put(dpy, 1, packed=packed)
    start(cheb_exchange(1))
    strips += wide_sweep(2, strips[1])

    halo = tuple((strips[0][h] + strips[1][h]) + (strips[2][h] + strips[3][h]) for h in range(2))
    for x in range(-1, BX + 1):
        m[x + 1] = (d[0, x + 2] + d[1, x + 2]) + (d[2, x + 2] + d[3, x + 2])
    for x in range(BX):
        value = m[x + 1]
        total = grad[x]
        for i, near in enumerate(row_sides(lambda y: m[y + 1], x, unpack_row(halo, x))):
            total = total - kk[i, x] * (value - near)
        grad[x] = total
        copy = pltpu.make_async_copy(grad.at[x], grad_h.at[:, x, :], in_sems.at[1, x])
        copy.start()
        writes.append(copy)

    for group in [perm_rows, press_rows, head_columns, conc_rows, conc_columns, area_columns,
                  flag_rows, flag_columns, tau_rows, tau_columns] + area_rows:
        for copy in group:
            copy.wait_send()
    for e in range(2):
        for copy in cheb_exchange(e):
            copy.wait_send()

    @pl.loop(0, ROUNDS * SPEC)
    def _(i):
        e = i // SPEC
        for copy in exchange(e, 2 * e, i % SPEC):
            copy.wait_send()

    for copy in writes:
        copy.wait()


def hand_over(adj, grad, adj_out, grad_out, adj_there, grad_there, sems):
    parts = [(adj.at[s], adj_there.at[s], adj_out.at[s]) for s in range(SPEC)] + [(grad, grad_there, grad_out)]
    inward = [pltpu.make_async_copy(a, b, sems.at[0, i]) for i, (a, b, c) in enumerate(parts)]
    outward = [pltpu.make_async_copy(b, c, sems.at[1, i]) for i, (a, b, c) in enumerate(parts)]
    for copy in inward:
        copy.start()
    for first, second in zip(inward, outward):
        first.wait()
        second.start()
    for copy in outward:
        copy.wait()


def body(adjoint_in, conc, pressure, perm, porosity, storage, rock, upwind, sorption):
    def vmem(*shape, dtype=F32):
        return pltpu.VMEM(shape, dtype)

    row = (NZ, LANES)
    tile = (8, LANES)
    hbm = pl.BlockSpec(memory_space=pltpu.HBM)
    adjoint_out, grad = pl.pallas_call(
        kernel,
        out_shape=(
            jax.ShapeDtypeStruct(adjoint_in.shape, F32),
            jax.ShapeDtypeStruct(pressure.shape, F32),
        ),
        in_specs=[hbm] * 8 + [hbm],
        out_specs=(hbm, hbm),
        scratch_shapes=[
            vmem(BX, SPEC, *row),
            vmem(BX + 2, SPEC, *row),
            vmem(BX + 4, *row),
            vmem(BX + 4, *row),
            vmem(BX, *row),
            vmem(BX, *row),
            vmem(BX, *row, dtype=jnp.int32),
            vmem(BX + 2, 4, *row, dtype=jnp.int32),
            vmem(BX + 2, SPEC, *row),
            vmem(SUB, BX + 4, SPEC, *row),
            vmem(BX + 2, SPEC, *row),
            vmem(ROUNDS, SPEC, 2, *tile),
            vmem(ROUNDS, SPEC, 2, *tile),
            vmem(ROUNDS, SPEC, 2, *tile),
            vmem(SPEC, 2, *tile),
            vmem(ROUNDS, SPEC, 4, *tile),
        ] + [vmem(2, 2, *tile)] * 3 + [
        ] + [vmem(SPEC, 2, *tile)] * 10 + [
            vmem(2, 4, *tile),
        ] + [vmem(6, 2, *tile)] * 3 + [
            vmem(BX + 2, 5, *row),
            vmem(4, BX, *row),
            vmem(BX + 2, 6, *row),
            vmem(4, BX, *row),
            vmem(6, BX, *row),
            vmem(CHEB, BX + 4, *row),
            vmem(2, 2, *tile),
            vmem(2, 2, *tile),
            vmem(2, 2, *tile),
            vmem(2, 4, *tile),
            vmem(BX + 2, *row),
            vmem(BX, *row),
            vmem(BX, *row),
            pltpu.SMEM((2, SPEC, ROCKS), F32),
            pltpu.SemaphoreType.DMA((11, BX)),
            pltpu.SemaphoreType.DMA((SLOTS, 8)),
            pltpu.SemaphoreType.DMA((SLOTS, 8)),
        ],
        compiler_params=pltpu.CompilerParams(
            collective_id=0, has_side_effects=True, vmem_limit_bytes=63 * 2**20),
    )(adjoint_in, conc, pressure, perm, porosity, storage, rock, upwind, jnp.transpose(sorption, (0, 2, 1)))
    return tuple(pl.pallas_call(
        hand_over,
        out_shape=(
            jax.ShapeDtypeStruct(adjoint_in.shape, F32),
            jax.ShapeDtypeStruct(pressure.shape, F32),
        ),
        in_specs=[hbm] * 2,
        out_specs=(hbm, hbm),
        scratch_shapes=[
            vmem(*adjoint_in.shape),
            vmem(*pressure.shape),
            pltpu.SemaphoreType.DMA((2, SPEC + 1)),
        ],
        compiler_params=pltpu.CompilerParams(vmem_limit_bytes=63 * 2**20),
    )(adjoint_out, grad))


def solution(mesh):
    in_specs = (
        P(None, None, "gx", "gy"),
        P(None, None, "gx", "gy"),
        P(None, "gx", "gy"),
        P(None, "gx", "gy"),
        P(None, "gx", "gy"),
        P(None, "gx", "gy"),
        P(None, "gx", "gy"),
        P(None, None, "gx", "gy"),
        P(),
    )
    out_specs = (P(None, None, "gx", "gy"), P(None, "gx", "gy"))
    return jax.shard_map(body, mesh=mesh, in_specs=in_specs, out_specs=out_specs, check_vma=False)
```
